32 devices in a mesh: grp: 2 (over x), rcv: 16 (over z, y, core).
Axes of the slice: x: 2, y: 2, z: 4, core: 2. Of those that a mesh axis runs over, the one named last changes fastest.
Arguments:
- records: bfloat16 [8, 1024, 2048], P('grp', 'rcv'), parts along dimension 0, may hold values from -40 to 40, as said below
- quality: int32 [8, 1024], P('grp', 'rcv'), parts along dimension 0, may hold values 0 or 1
- block_ids: int32 [4], P('grp'), parts along dimension 0, may hold values from 0 to 15, as said below
Outputs:
- stacked: bfloat16 [16, 64, 128, 1024], P('rcv', 'grp'), parts along dimension 1
The draws below stay inside these ranges and needn't reach their ends.
There are 2 independent parts, one for each index of `grp`. The reference program is written for one: setup_inputs(seed, part) draws one part's arguments, and reference() takes and returns one part's arrays. A program takes and returns all parts, laid end to end along the dimension named above; each array names one. Nothing has to cross between parts.
Inputs may be any that keep to these rules, and one draw needn't show every extreme that they name: records hold finite samples. `block_ids`: 2 distinct block numbers.
All inputs are finite; a program needn't handle non-finite values. No bound on the sum of `quality` on one device may be relied on, other than what follows from the above.
Results may differ from the reference program's by a relative error of at most 0.0066.
Values may be sent and summed in bfloat16 or wider, within the bound.
A program may use at most 64 MiB of HBM per device.

```python
import jax
import jax.numpy as jnp
from jax import lax

S = 2048
NB = 8
BIN = 32
FLO = 64
CH_DEV = 64
W = 4
SBLK = 64
NSB = 2
CH = 1024
N_RCV = 16


def draw_records(key, part):
    key_scale = jax.random.fold_in(key, 11)
    key_noise = jax.random.fold_in(key, 12)
    scales = jnp.exp(jax.random.uniform(key_scale, (W, CH, 1), jnp.float32, 0.0, jnp.log(10.0)))
    noise_part = jax.random.normal(key_noise, (W, CH, S), jnp.float32)
    return jnp.clip(noise_part * scales, -40.0, 40.0).astype(jnp.bfloat16)


def draw_block_ids(key, part):
    shuffled = jax.random.permutation(jax.random.fold_in(key, 21), CH // SBLK)
    return shuffled[:NSB].astype(jnp.int32)


def plant(array, key, low, largest):
    shape = array.shape
    spot = [jax.random.randint(jax.random.fold_in(key, axis), (), 0, shape[axis]) for axis in range(len(shape))]
    array = array.at[tuple(spot)].set(low)
    longest = shape.index(max(shape))
    spot[longest] = (spot[longest] + 1) % shape[longest]
    return array.at[tuple(spot)].set(largest)


def setup_inputs(seed: int = 0, part: int = 0) -> dict:
    splits = jax.random.split(jax.random.key(seed), 4)
    part_keys = jax.random.split(jax.random.fold_in(splits[3], part), 4)
    records = draw_records(jax.random.fold_in(jax.random.fold_in(splits[3], part), 71), part)
    quality = plant((jax.random.randint(part_keys[1], (W, CH), 0, 8) < 7).astype(jnp.int32), jax.random.fold_in(part_keys[1], 1), 0, 1)
    block_ids = draw_block_ids(jax.random.fold_in(jax.random.fold_in(splits[3], part), 71), part)
    return {"records": records, "quality": quality, "block_ids": block_ids}


def make_basis(samples):
    times = jnp.arange(samples, dtype=jnp.int32)
    bins_all = FLO + jnp.arange(NB * BIN, dtype=jnp.int32)
    phases = times[:, None] * bins_all[None, :] % samples
    angles = phases.astype(jnp.float32) * (2.0 * jnp.pi / samples)
    cosine = jnp.cos(angles).reshape(samples, NB, 1, BIN)
    sine_neg = (-jnp.sin(angles)).reshape(samples, NB, 1, BIN)
    return jnp.concatenate([cosine, sine_neg], axis=2).reshape(samples, NB * 2 * BIN).astype(jnp.bfloat16)

def reference(records, quality, block_ids):
    windows, channels, samples = records.shape
    basis_table = make_basis(samples)
    spectrum = jnp.dot(records.reshape(windows * channels, samples), basis_table, preferred_element_type=jnp.float32)
    spectrum = spectrum.reshape(windows, channels, NB, 2 * BIN)
    band_power = lax.optimization_barrier(jnp.sum(spectrum * spectrum, axis=-1)) / BIN
    scaling = quality[:, :, None].astype(jnp.float32) * lax.rsqrt(band_power + 1e-05)
    whitened = (spectrum * scaling[..., None]).astype(jnp.bfloat16)
    offsets = jnp.arange(SBLK, dtype=jnp.int32)
    chosen = (block_ids[:, None].astype(jnp.int32) * SBLK + offsets[None, :]).reshape(-1).astype(jnp.int32)
    sources = jnp.take(whitened, chosen, axis=1)
    groups = N_RCV // NB
    sub_rows = CH_DEV // groups
    grouped = whitened.reshape(windows, N_RCV, groups, sub_rows, NB, 2, BIN)
    source_count = chosen.shape[0]

    def per_band(band_index):
        src_band = lax.dynamic_index_in_dim(sources, band_index, 2, keepdims=False)
        src_band = src_band.reshape(windows, source_count, 2, BIN).astype(jnp.float32)
        recv_band = lax.dynamic_index_in_dim(grouped, band_index, 4, keepdims=False).astype(jnp.float32)
        products = jnp.einsum('wnpi,wsqjri->qinprsj', src_band, recv_band)
        real_part = products[:, :, :, 0, 0] + products[:, :, :, 1, 1]
        imag_part = products[:, :, :, 0, 1] - products[:, :, :, 1, 0]
        real_part = real_part.reshape(groups, BIN, source_count, N_RCV * sub_rows)
        imag_part = imag_part.reshape(groups, BIN, source_count, N_RCV * sub_rows)
        joined = jnp.concatenate([real_part, imag_part], axis=-1)
        return (joined * (1.0 / windows)).astype(jnp.bfloat16)
    result = lax.map(per_band, jnp.arange(NB, dtype=jnp.int32))
    return result.reshape(NB * groups, BIN, source_count, 2 * N_RCV * sub_rows)
```

```python
import functools

import jax
import jax.numpy as jnp
import ml_dtypes
import numpy as np
from jax import lax
from jax.experimental import pallas as pl
from jax.experimental.pallas import tpu as pltpu
from jax.sharding import PartitionSpec as P

NB = 8
BIN = 32
FLO = 64
SBLK = 64
NSB = 2
LANES = 128


def basis_rows(samples, count):
    times = np.arange(count, dtype=np.int64)
    bins = FLO + np.arange(NB * BIN, dtype=np.int64)
    phases = (bins[:, None] * times[None, :]) % samples
    angles = phases.astype(np.float64) * (2.0 * np.pi / samples)
    table = np.stack([np.cos(angles), -np.sin(angles)]).reshape(2, NB, BIN, count)
    table = table.transpose(1, 0, 2, 3).reshape(NB * 2 * BIN, count)
    return table.astype(np.float32).astype(ml_dtypes.bfloat16)


def lanes_to_rows(pieces, width):
    lane = lax.broadcasted_iota(jnp.int32, pieces[0].shape, 1) // width
    wide = [piece.astype(jnp.float32) for piece in pieces]
    result = []
    for w in range(len(pieces)):
        total = None
        for e, piece in enumerate(wide):
            shift = (e - w) * width % LANES
            moved = pltpu.roll(piece, shift, 1) if shift else piece
            total = moved if total is None else jnp.where(lane == e, moved, total)
        result.append(total)
    return result


def flipped(me, off):
    other, bit = me, 1
    while bit <= off:
        if off & bit:
            other = other + bit * (1 - 2 * (me // bit % 2))
        bit *= 2
    return other


def exchange_kernel(
    ids_ref, quality_ref, basis_ref, records_ref, rhs_ref, src_ref,
    basis_v, rec_v, send_v, recv_v, rhs_v, own_v,
    load_sem, send_sem, recv_sem, plane_sem, src_sem,
):
    devices = recv_v.shape[0]
    windows, channels, samples = records_ref.shape
    groups = devices // NB
    sub_rows = channels // groups
    pack = LANES // sub_rows
    planes = devices // pack
    half = samples // 2
    rows = 2 * BIN
    me = lax.axis_index("rcv")

    loads = [pltpu.make_async_copy(basis_ref, basis_v, load_sem.at[0])]
    for q in range(groups):
        for w in range(windows):
            place = q * windows + w
            loads.append(
                pltpu.make_async_copy(
                    records_ref.at[w, pl.ds(q * sub_rows, sub_rows)],
                    rec_v.at[pl.ds(place * sub_rows, sub_rows)],
                    load_sem.at[1 + place],
                )
            )
    for load in loads:
        load.start()

    barrier = pltpu.get_barrier_semaphore()
    for off in range(1, devices):
        pl.semaphore_signal(
            barrier, inc=1, device_id={"rcv": flipped(me, off)},
            device_id_type=pl.DeviceIdType.MESH,
        )

    keep = jnp.concatenate(
        [
            quality_ref[w : w + 1, q * sub_rows : (q + 1) * sub_rows]
            for q in range(groups)
            for w in range(windows)
        ],
        axis=1,
    ).astype(jnp.float32)
    for load in loads:
        load.wait()

    contract = (((1,), (1,)), ((), ()))
    low = lax.dot_general(
        basis_v[...], rec_v[:, :half], contract, preferred_element_type=jnp.float32
    )
    high = lax.dot_general(
        basis_v[...], rec_v[:, half:], contract, preferred_element_type=jnp.float32
    )
    odd = lax.broadcasted_iota(jnp.int32, (rows, low.shape[1]), 0) % 2 == 1
    for b in range(NB):
        band = slice(b * rows, (b + 1) * rows)
        spectrum = low[band] + jnp.where(odd, -high[band], high[band])
        power = jnp.sum(spectrum * spectrum, axis=0, keepdims=True) / BIN
        white = (spectrum * (keep * lax.rsqrt(power + 1e-05))).astype(jnp.bfloat16)
        for q in range(groups):
            send_v[b * groups + q] = white[:, q * LANES : (q + 1) * LANES]

    pl.semaphore_wait(barrier, devices - 1)
    copies = {}
    for off in range(devices - 1, 0, -1):
        peer = flipped(me, off)
        copies[off] = pltpu.make_async_remote_copy(
            src_ref=send_v.at[peer], dst_ref=recv_v.at[me],
            send_sem=send_sem.at[off], recv_sem=recv_sem.at[off],
            device_id={"rcv": peer}, device_id_type=pl.DeviceIdType.MESH,
        )
        copies[off].start()
    recv_v[me] = send_v[me]

    outs = []
    for dz in range(planes):
        plane = flipped(me // pack, dz)
        for e in range(pack):
            off = dz * pack + e
            if off:
                copies[off].wait_recv()
        if dz == planes - 1:
            for s in range(NSB):
                own_v[s] = recv_v[ids_ref[s]]
            swap = pltpu.make_async_remote_copy(
                src_ref=own_v, dst_ref=src_ref.at[me % groups],
                send_sem=src_sem.at[0], recv_sem=src_sem.at[1],
                device_id={"rcv": flipped(me, 1)}, device_id_type=pl.DeviceIdType.MESH,
            )
            swap.start()
            keep_own = pltpu.make_async_copy(own_v, src_ref.at[me % groups], src_sem.at[2])
            keep_own.start()
        by_window = lanes_to_rows([recv_v[plane * pack + e] for e in range(pack)], sub_rows)
        for w, block in enumerate(by_window):
            real, imag = block[:BIN], block[BIN:]
            rhs_v[0, plane, w * rows : w * rows + BIN] = real.astype(jnp.bfloat16)
            rhs_v[0, plane, w * rows + BIN : (w + 1) * rows] = imag.astype(jnp.bfloat16)
            rhs_v[1, plane, w * rows : w * rows + BIN] = imag.astype(jnp.bfloat16)
            rhs_v[1, plane, w * rows + BIN : (w + 1) * rows] = (-real).astype(jnp.bfloat16)
        for part in range(2):
            out = pltpu.make_async_copy(
                rhs_v.at[part, plane], rhs_ref.at[part, plane], plane_sem.at[part, dz]
            )
            out.start()
            outs.append(out)
    for off in range(devices - 1, 0, -1):
        copies[off].wait_send()
    for out in outs:
        out.wait()
    keep_own.wait()
    swap.wait()


def product_kernel(src_ref, rhs_ref, out_ref, left_v):
    step = pl.program_id(0)
    bins = out_ref.shape[0]
    rows = 2 * BIN
    windows = rhs_ref.shape[2] // rows
    groups, blocks = src_ref.shape[:2]
    sub_rows = SBLK // groups

    @pl.when(step == 0)
    def _():
        pieces = [src_ref[q, s] for s in range(blocks) for q in range(groups)]
        by_window = lanes_to_rows(pieces, sub_rows)
        left_v[...] = jnp.concatenate(by_window, axis=0).T * (1.0 / windows)

    left = left_v[...]
    bin_of = lax.broadcasted_iota(jnp.int32, left.shape, 1) % BIN
    masked = jnp.concatenate(
        [jnp.where(bin_of == step * bins + i, left, 0.0).astype(jnp.bfloat16) for i in range(bins)],
        axis=0,
    )
    planes = rhs_ref.shape[1]
    wide = 2
    for part in range(2):
        for z in range(0, planes, wide):
            right = jnp.concatenate([rhs_ref[part, z + u] for u in range(wide)], axis=1)
            both = jnp.dot(masked, right, preferred_element_type=jnp.float32)
            first = (part * planes + z) * LANES
            out_ref[:, :, first : first + wide * LANES] = both.astype(jnp.bfloat16).reshape(
                bins, left.shape[0], wide * LANES
            )


def per_device_kernels(records, quality, block_ids):
    devices = lax.axis_size("rcv")
    groups = devices // NB
    windows, channels, samples = records.shape
    sub_rows = channels // groups
    pack = LANES // sub_rows
    planes = devices // pack
    rows = 2 * BIN
    depth = windows * rows
    basis = jnp.asarray(basis_rows(samples, samples // 2))
    rhs, src = pl.pallas_call(
        exchange_kernel,
        out_shape=(
            jax.ShapeDtypeStruct((2, planes, depth, LANES), jnp.bfloat16),
            jax.ShapeDtypeStruct((groups, NSB, rows, LANES), jnp.bfloat16),
        ),
        in_specs=[
            pl.BlockSpec(memory_space=pltpu.SMEM),
            pl.BlockSpec(memory_space=pltpu.VMEM),
            pl.BlockSpec(memory_space=pl.ANY),
            pl.BlockSpec(memory_space=pl.ANY),
        ],
        out_specs=(pl.BlockSpec(memory_space=pl.ANY), pl.BlockSpec(memory_space=pl.ANY)),
        scratch_shapes=[
            pltpu.VMEM(basis.shape, jnp.bfloat16),
            pltpu.VMEM((windows * channels, samples), jnp.bfloat16),
            pltpu.VMEM((devices, rows, LANES), jnp.bfloat16),
            pltpu.VMEM((devices, rows, LANES), jnp.bfloat16),
            pltpu.VMEM((2, planes, depth, LANES), jnp.bfloat16),
            pltpu.VMEM((NSB, rows, LANES), jnp.bfloat16),
            pltpu.SemaphoreType.DMA((1 + groups * windows,)),
            pltpu.SemaphoreType.DMA((devices,)),
            pltpu.SemaphoreType.DMA((devices,)),
            pltpu.SemaphoreType.DMA((2, planes)),
            pltpu.SemaphoreType.DMA((3,)),
        ],
        compiler_params=pltpu.CompilerParams(
            collective_id=0, has_side_effects=True, vmem_limit_bytes=32 * 2**20
        ),
        name="spectra_exchange",
    )(block_ids, quality, basis, records)

    count = NSB * SBLK
    step_bins = 4
    joined = pl.pallas_call(
        product_kernel,
        grid=(BIN // step_bins,),
        out_shape=jax.ShapeDtypeStruct((BIN, count, 2 * planes * LANES), jnp.bfloat16),
        in_specs=[
            pl.BlockSpec(src.shape, lambda i: (0, 0, 0, 0)),
            pl.BlockSpec(rhs.shape, lambda i: (0, 0, 0, 0)),
        ],
        out_specs=pl.BlockSpec((step_bins, count, 2 * planes * LANES), lambda i: (i, 0, 0)),
        scratch_shapes=[pltpu.VMEM((count, depth), jnp.float32)],
        compiler_params=pltpu.CompilerParams(vmem_limit_bytes=32 * 2**20),
        name="cross_spectra",
    )(src, rhs)
    return joined[None]


def make_basis(samples):
    return jnp.asarray(basis_rows(samples, samples).T)


def from_partner(value, axis, stride):
    mask = 2**stride
    pairs = [(source, source ^ mask) for source in range(lax.axis_size(axis))]
    return lax.ppermute(value, axis, pairs)


def per_device_general(records, quality, block_ids):
    devices = lax.axis_size("rcv")
    groups = devices // NB
    windows, channels, samples = records.shape
    sub_rows = channels // groups
    basis_table = make_basis(samples).reshape(samples, NB, 2 * BIN)
    rec_rows = records.reshape(windows, groups, sub_rows, samples)
    spectrum = jnp.einsum(
        "wqjs,sbm->bqwjm", rec_rows, basis_table, preferred_element_type=jnp.float32
    )
    band_power = jnp.sum(spectrum * spectrum, axis=-1) / BIN
    keep_gate = quality.reshape(windows, groups, sub_rows).transpose(1, 0, 2).astype(jnp.float32)
    scaling = keep_gate[None] * lax.rsqrt(band_power + 1e-05)
    whitened = (spectrum * scaling[..., None]).astype(jnp.bfloat16)
    send_buf = whitened.reshape(devices, windows, sub_rows * 2 * BIN)
    arrived = lax.all_to_all(send_buf, "rcv", split_axis=0, concat_axis=0, tiled=True)
    receivers = arrived.reshape(devices, windows, sub_rows, 2, BIN)
    my_index = lax.axis_index("rcv")
    per_block = channels // SBLK
    blk_rows = SBLK // sub_rows
    own_pieces = []
    for source_slot in range(NSB):
        owner_dev = block_ids[source_slot] // per_block
        own_pieces.append(lax.dynamic_index_in_dim(arrived, owner_dev, 0, keepdims=False))
    collected = jnp.stack(own_pieces)[None]
    my_group = my_index % groups
    for bit_level in range(groups.bit_length() - 1):
        partner = from_partner(collected, "rcv", bit_level)
        upper_side = my_group // 2**bit_level % 2 == 1
        low_half = jnp.where(upper_side, partner, collected)
        high_half = jnp.where(upper_side, collected, partner)
        collected = jnp.concatenate([low_half, high_half], axis=0)
    slices = []
    for source_slot in range(NSB):
        slices.append(collected[:, source_slot])
    src_band = jnp.stack(slices).reshape(NSB, blk_rows, windows, sub_rows, 2, BIN)
    source_count = NSB * SBLK
    group_width = devices * sub_rows
    left_side = src_band.transpose(5, 0, 1, 3, 2, 4).reshape(BIN, source_count, windows, 2)
    rec_cols = receivers.transpose(4, 1, 3, 0, 2).reshape(BIN, windows, 2, group_width)
    rotated = jnp.stack([rec_cols[:, :, 1], -rec_cols[:, :, 0]], axis=2)
    right_side = jnp.concatenate([rec_cols, rotated], axis=-1)
    joined = jnp.einsum("inwp,iwpk->ink", left_side, right_side, preferred_element_type=jnp.float32)
    return (joined * (1.0 / windows)).astype(jnp.bfloat16)[None]


def per_device(records, quality, block_ids):
    devices = lax.axis_size("rcv")
    windows, channels, samples = records.shape
    groups = devices // NB
    sub_rows = channels // groups
    pack = LANES // sub_rows
    fits = (
        groups == 2
        and channels == SBLK
        and windows == pack
        and sub_rows * pack == LANES
        and NSB * groups == pack
        and devices % (2 * pack) == 0
        and FLO % 2 == 0
        and samples % 2 == 0
    )
    return (per_device_kernels if fits else per_device_general)(records, quality, block_ids)


def solution(mesh):
    placed = (P("grp", "rcv", None), P("grp", "rcv"), P("grp"))
    return jax.shard_map(
        per_device,
        mesh=mesh,
        in_specs=placed,
        out_specs=P("rcv", "grp", None, None),
        check_vma=False,
    )
```

```python
import functools

import jax
import jax.numpy as jnp
import ml_dtypes
import numpy as np
from jax import lax
from jax.experimental import pallas as pl
from jax.experimental.pallas import tpu as pltpu
from jax.sharding import PartitionSpec as P

NB = 8
BIN = 32
FLO = 64
SBLK = 64
NSB = 2
LANES = 128


def basis_rows(samples, count):
    times = np.arange(count, dtype=np.int64)
    bins = FLO + np.arange(NB * BIN, dtype=np.int64)
    phases = (bins[:, None] * times[None, :]) % samples
    angles = phases.astype(np.float64) * (2.0 * np.pi / samples)
    table = np.stack([np.cos(angles), -np.sin(angles)]).reshape(2, NB, BIN, count)
    table = table.transpose(1, 0, 2, 3).reshape(NB * 2 * BIN, count)
    return table.astype(np.float32).astype(ml_dtypes.bfloat16)


def lanes_to_rows(pieces, width):
    lane = lax.broadcasted_iota(jnp.int32, pieces[0].shape, 1) // width
    wide = [piece.astype(jnp.float32) for piece in pieces]
    result = []
    for w in range(len(pieces)):
        total = None
        for e, piece in enumerate(wide):
            shift = (e - w) * width % LANES
            moved = pltpu.roll(piece, shift, 1) if shift else piece
            total = moved if total is None else jnp.where(lane == e, moved, total)
        result.append(total)
    return result


def flipped(me, off):
    other, bit = me, 1
    while bit <= off:
        if off & bit:
            other = other + bit * (1 - 2 * (me // bit % 2))
        bit *= 2
    return other


def exchange_kernel(
    small_ref, basis_ref, records_ref, rhs_ref, src_ref,
    basis_v, rec_v, send_v, recv_v, own_v,
    load_sem, basis_sem, send_sem, recv_sem, src_sem,
):
    devices = recv_v.shape[0]
    windows, channels, samples = records_ref.shape
    groups = devices // NB
    sub_rows = channels // groups
    pack = LANES // sub_rows
    planes = devices // pack
    half = samples // 2
    rows = 2 * BIN
    me = lax.axis_index("rcv")

    barrier = pltpu.get_barrier_semaphore()
    for off in range(1, devices):
        pl.semaphore_signal(
            barrier, inc=1, device_id={"rcv": flipped(me, off)},
            device_id_type=pl.DeviceIdType.MESH,
        )

    loads = []
    for q in range(groups):
        for w in range(windows):
            place = q * windows + w
            loads.append(
                pltpu.make_async_copy(
                    records_ref.at[w, pl.ds(q * sub_rows, sub_rows)],
                    rec_v.at[pl.ds(place * sub_rows, sub_rows)],
                    load_sem.at[place],
                )
            )
    near_side = me // (devices // 2)
    sides = (1 - near_side, near_side)
    side_rows = NB * rows // 2
    basis_loads = []
    for turn, side in enumerate(sides):
        piece = pl.ds(pl.multiple_of(side * side_rows, side_rows), side_rows)
        basis_loads.append(
            pltpu.make_async_copy(basis_ref.at[piece], basis_v.at[turn], basis_sem.at[turn])
        )
    for load in loads + basis_loads:
        load.start()
    for load in loads:
        load.wait()

    keep = jnp.concatenate(
        [
            small_ref[w : w + 1, q * sub_rows : (q + 1) * sub_rows]
            for q in range(groups)
            for w in range(windows)
        ],
        axis=1,
    ).astype(jnp.float32)
    contract = (((1,), (1,)), ((), ()))
    odd = lax.broadcasted_iota(jnp.int32, (rows, keep.shape[1]), 0) % 2 == 1
    copies = {}
    for turn, side in enumerate(sides):
        basis_loads[turn].wait()
        low = lax.dot_general(
            basis_v[turn], rec_v[:, :half], contract, preferred_element_type=jnp.float32
        )
        high = lax.dot_general(
            basis_v[turn], rec_v[:, half:], contract, preferred_element_type=jnp.float32
        )
        for b in range(NB // 2):
            band = slice(b * rows, (b + 1) * rows)
            spectrum = low[band] + jnp.where(odd, -high[band], high[band])
            power = jnp.sum(spectrum * spectrum, axis=0, keepdims=True) / BIN
            white = (spectrum * (keep * lax.rsqrt(power + 1e-05))).astype(jnp.bfloat16)
            for q in range(groups):
                send_v[side * (devices // 2) + b * groups + q] = white[:, q * LANES : (q + 1) * LANES]
        if turn == 0:
            pl.semaphore_wait(barrier, devices - 1)
        offs = range(devices // 2, devices) if turn == 0 else range(1, devices // 2)
        for off in reversed(offs):
            peer = flipped(me, off)
            copies[off] = pltpu.make_async_remote_copy(
                src_ref=send_v.at[peer], dst_ref=recv_v.at[me],
                send_sem=send_sem.at[off], recv_sem=recv_sem.at[off],
                device_id={"rcv": peer}, device_id_type=pl.DeviceIdType.MESH,
            )
            copies[off].start()
    recv_v[me] = send_v[me]

    for dz in range(planes):
        plane = flipped(me // pack, dz)
        for e in range(pack):
            off = dz * pack + e
            if off:
                copies[off].wait_recv()
        if dz == planes - 1:
            for s in range(NSB):
                own_v[s] = recv_v[small_ref[0, channels + s]]
            swap = pltpu.make_async_remote_copy(
                src_ref=own_v, dst_ref=src_ref.at[me % groups],
                send_sem=src_sem.at[0], recv_sem=src_sem.at[1],
                device_id={"rcv": flipped(me, 1)}, device_id_type=pl.DeviceIdType.MESH,
            )
            swap.start()
            src_ref[me % groups] = own_v[...]
        by_window = lanes_to_rows([recv_v[plane * pack + e] for e in range(pack)], sub_rows)
        for w, block in enumerate(by_window):
            real, imag = block[:BIN], block[BIN:]
            rhs_ref[0, plane, w * rows : w * rows + BIN] = real.astype(jnp.bfloat16)
            rhs_ref[0, plane, w * rows + BIN : (w + 1) * rows] = imag.astype(jnp.bfloat16)
            rhs_ref[1, plane, w * rows : w * rows + BIN] = imag.astype(jnp.bfloat16)
            rhs_ref[1, plane, w * rows + BIN : (w + 1) * rows] = (-real).astype(jnp.bfloat16)
    for off in range(devices - 1, 0, -1):
        copies[off].wait_send()
    swap.wait()


STEP_BINS = 4


def product_kernel(src_ref, rhs_ref, out_ref, left_v, out_v, out_sem):
    rows = 2 * BIN
    planes = rhs_ref.shape[1]
    windows = rhs_ref.shape[2] // rows
    groups, blocks = src_ref.shape[:2]
    sub_rows = SBLK // groups
    wide = 2

    pieces = [src_ref[q, s] for s in range(blocks) for q in range(groups)]
    by_window = lanes_to_rows(pieces, sub_rows)
    left_v[...] = jnp.concatenate(by_window, axis=0).T * (1.0 / windows)

    def write(place):
        return pltpu.make_async_copy(out_v.at[place], out_ref.at[place], out_sem.at[place])

    def step_body(step, carry):
        left = left_v[...]
        bin_of = lax.broadcasted_iota(jnp.int32, left.shape, 1) % BIN
        masked = jnp.concatenate(
            [
                jnp.where(bin_of == step * STEP_BINS + i, left, 0.0).astype(jnp.bfloat16)
                for i in range(STEP_BINS)
            ],
            axis=0,
        )
        for part in range(2):
            for z in range(0, planes, wide):
                right = jnp.concatenate([rhs_ref[part, z + u] for u in range(wide)], axis=1)
                both = jnp.dot(masked, right, preferred_element_type=jnp.float32)
                first = (part * planes + z) * LANES
                out_v[pl.ds(step * STEP_BINS, STEP_BINS), :, first : first + wide * LANES] = (
                    both.astype(jnp.bfloat16).reshape(STEP_BINS, left.shape[0], wide * LANES)
                )
        for i in range(STEP_BINS):
            write(step * STEP_BINS + i).start()
        return carry

    lax.fori_loop(0, BIN // STEP_BINS, step_body, 0)

    def wait_body(place, carry):
        write(place).wait()
        return carry

    lax.fori_loop(0, BIN, wait_body, 0)


def per_device_kernels(records, quality, block_ids):
    devices = lax.axis_size("rcv")
    groups = devices // NB
    windows, channels, samples = records.shape
    sub_rows = channels // groups
    pack = LANES // sub_rows
    planes = devices // pack
    rows = 2 * BIN
    depth = windows * rows
    basis = jnp.asarray(basis_rows(samples, samples // 2))
    padded_ids = jnp.pad(block_ids.reshape(1, -1), ((0, windows - 1), (0, LANES - channels - NSB)))
    small = jnp.concatenate([quality, padded_ids], axis=1)
    rhs, src = pl.pallas_call(
        exchange_kernel,
        out_shape=(
            jax.ShapeDtypeStruct((2, planes, depth, LANES), jnp.bfloat16),
            jax.ShapeDtypeStruct((groups, NSB, rows, LANES), jnp.bfloat16),
        ),
        in_specs=[
            pl.BlockSpec(memory_space=pltpu.VMEM),
            pl.BlockSpec(memory_space=pltpu.HBM),
            pl.BlockSpec(memory_space=pltpu.HBM),
        ],
        out_specs=(pl.BlockSpec(memory_space=pltpu.VMEM), pl.BlockSpec(memory_space=pltpu.VMEM)),
        scratch_shapes=[
            pltpu.VMEM((2, basis.shape[0] // 2, basis.shape[1]), jnp.bfloat16),
            pltpu.VMEM((windows * channels, samples), jnp.bfloat16),
            pltpu.VMEM((devices, rows, LANES), jnp.bfloat16),
            pltpu.VMEM((devices, rows, LANES), jnp.bfloat16),
            pltpu.VMEM((NSB, rows, LANES), jnp.bfloat16),
            pltpu.SemaphoreType.DMA((groups * windows,)),
            pltpu.SemaphoreType.DMA((2,)),
            pltpu.SemaphoreType.DMA((devices,)),
            pltpu.SemaphoreType.DMA((devices,)),
            pltpu.SemaphoreType.DMA((2,)),
        ],
        compiler_params=pltpu.CompilerParams(
            collective_id=0, has_side_effects=True, vmem_limit_bytes=53 * 2**20
        ),
        name="spectra_exchange",
    )(small, basis, records)

    count = NSB * SBLK
    out_shape = (BIN, count, 2 * planes * LANES)
    joined = pl.pallas_call(
        product_kernel,
        out_shape=jax.ShapeDtypeStruct(out_shape, jnp.bfloat16),
        in_specs=[pl.BlockSpec(memory_space=pltpu.VMEM)] * 2,
        out_specs=pl.BlockSpec(memory_space=pltpu.HBM),
        scratch_shapes=[
            pltpu.VMEM((count, depth), jnp.float32),
            pltpu.VMEM(out_shape, jnp.bfloat16),
            pltpu.SemaphoreType.DMA((BIN,)),
        ],
        compiler_params=pltpu.CompilerParams(vmem_limit_bytes=40 * 2**20),
        name="cross_spectra",
    )(src, rhs)
    return joined[None]


def make_basis(samples):
    return jnp.asarray(basis_rows(samples, samples).T)


def from_partner(value, axis, stride):
    mask = 2**stride
    pairs = [(source, source ^ mask) for source in range(lax.axis_size(axis))]
    return lax.ppermute(value, axis, pairs)


def per_device_general(records, quality, block_ids):
    devices = lax.axis_size("rcv")
    groups = devices // NB
    windows, channels, samples = records.shape
    sub_rows = channels // groups
    basis_table = make_basis(samples).reshape(samples, NB, 2 * BIN)
    rec_rows = records.reshape(windows, groups, sub_rows, samples)
    spectrum = jnp.einsum(
        "wqjs,sbm->bqwjm", rec_rows, basis_table, preferred_element_type=jnp.float32
    )
    band_power = jnp.sum(spectrum * spectrum, axis=-1) / BIN
    keep_gate = quality.reshape(windows, groups, sub_rows).transpose(1, 0, 2).astype(jnp.float32)
    scaling = keep_gate[None] * lax.rsqrt(band_power + 1e-05)
    whitened = (spectrum * scaling[..., None]).astype(jnp.bfloat16)
    send_buf = whitened.reshape(devices, windows, sub_rows * 2 * BIN)
    arrived = lax.all_to_all(send_buf, "rcv", split_axis=0, concat_axis=0, tiled=True)
    receivers = arrived.reshape(devices, windows, sub_rows, 2, BIN)
    my_index = lax.axis_index("rcv")
    per_block = channels // SBLK
    blk_rows = SBLK // sub_rows
    own_pieces = []
    for source_slot in range(NSB):
        owner_dev = block_ids[source_slot] // per_block
        own_pieces.append(lax.dynamic_index_in_dim(arrived, owner_dev, 0, keepdims=False))
    collected = jnp.stack(own_pieces)[None]
    my_group = my_index % groups
    for bit_level in range(groups.bit_length() - 1):
        partner = from_partner(collected, "rcv", bit_level)
        upper_side = my_group // 2**bit_level % 2 == 1
        low_half = jnp.where(upper_side, partner, collected)
        high_half = jnp.where(upper_side, collected, partner)
        collected = jnp.concatenate([low_half, high_half], axis=0)
    slices = []
    for source_slot in range(NSB):
        slices.append(collected[:, source_slot])
    src_band = jnp.stack(slices).reshape(NSB, blk_rows, windows, sub_rows, 2, BIN)
    source_count = NSB * SBLK
    group_width = devices * sub_rows
    left_side = src_band.transpose(5, 0, 1, 3, 2, 4).reshape(BIN, source_count, windows, 2)
    rec_cols = receivers.transpose(4, 1, 3, 0, 2).reshape(BIN, windows, 2, group_width)
    rotated = jnp.stack([rec_cols[:, :, 1], -rec_cols[:, :, 0]], axis=2)
    right_side = jnp.concatenate([rec_cols, rotated], axis=-1)
    joined = jnp.einsum("inwp,iwpk->ink", left_side, right_side, preferred_element_type=jnp.float32)
    return (joined * (1.0 / windows)).astype(jnp.bfloat16)[None]


def per_device(records, quality, block_ids):
    devices = lax.axis_size("rcv")
    windows, channels, samples = records.shape
    groups = devices // NB
    sub_rows = channels // groups
    pack = LANES // sub_rows
    fits = (
        groups == 2
        and channels == SBLK
        and windows == pack
        and sub_rows * pack == LANES
        and NSB * groups == pack
        and devices % (2 * pack) == 0
        and FLO % 2 == 0
        and samples % 2 == 0
    )
    return (per_device_kernels if fits else per_device_general)(records, quality, block_ids)


def solution(mesh):
    placed = (P("grp", "rcv", None), P("grp", "rcv"), P("grp"))
    return jax.shard_map(
        per_device,
        mesh=mesh,
        in_specs=placed,
        out_specs=P("rcv", "grp", None, None),
        check_vma=False,
    )
```

```python
import functools

import jax
import jax.numpy as jnp
import ml_dtypes
import numpy as np
from jax import lax
from jax.experimental import pallas as pl
from jax.experimental.pallas import tpu as pltpu
from jax.sharding import PartitionSpec as P

NB = 8
BIN = 32
FLO = 64
SBLK = 64
NSB = 2
LANES = 128


def basis_table(samples, count):
    times = np.arange(count, dtype=np.int64)
    bins = FLO + np.arange(NB * BIN, dtype=np.int64)
    phases = (times[:, None] * bins[None, :]) % samples
    angles = phases.astype(np.float64) * (2.0 * np.pi / samples)
    table = np.stack([np.cos(angles), -np.sin(angles)]).reshape(2, count, NB, BIN)
    table = table.transpose(1, 2, 0, 3).reshape(count, NB * 2 * BIN)
    return table.astype(np.float32).astype(ml_dtypes.bfloat16)


def lanes_to_rows(pieces, width):
    lane = lax.broadcasted_iota(jnp.int32, pieces[0].shape, 1) // width
    wide = [piece.astype(jnp.float32) for piece in pieces]
    result = []
    for w in range(len(pieces)):
        total = None
        for e, piece in enumerate(wide):
            shift = (e - w) * width % LANES
            moved = pltpu.roll(piece, shift, 1) if shift else piece
            total = moved if total is None else jnp.where(lane == e, moved, total)
        result.append(total)
    return result


def flipped(me, off):
    other, bit = me, 1
    while bit <= off:
        if off & bit:
            other = other + bit * (1 - 2 * (me // bit % 2))
        bit *= 2
    return other


def exchange_kernel(
    small_ref, basis_ref, records_ref, rhs_ref, src_ref,
    basis_v, rec_v, send_v, recv_v, own_v,
    load_sem, basis_sem, send_sem, recv_sem, src_sem,
):
    devices = recv_v.shape[0]
    windows, channels, samples = records_ref.shape
    groups = devices // NB
    sub_rows = channels // groups
    pack = LANES // sub_rows
    planes = devices // pack
    half = samples // 2
    rows = 2 * BIN
    me = lax.axis_index("rcv")

    barrier = pltpu.get_barrier_semaphore()
    for off in range(1, devices):
        pl.semaphore_signal(
            barrier, inc=1, device_id={"rcv": flipped(me, off)},
            device_id_type=pl.DeviceIdType.MESH,
        )

    loads = []
    for q in range(groups):
        for w in range(windows):
            place = q * windows + w
            for h in range(2):
                loads.append(
                    pltpu.make_async_copy(
                        records_ref.at[w, pl.ds(q * sub_rows, sub_rows), pl.ds(h * half, half)],
                        rec_v.at[h, pl.ds(place * sub_rows, sub_rows)],
                        load_sem.at[2 * place + h],
                    )
                )
    near_side = me // (devices // 2)
    sides = (1 - near_side, near_side)
    basis_loads = [
        pltpu.make_async_copy(basis_ref.at[side], basis_v.at[turn], basis_sem.at[turn])
        for turn, side in enumerate(sides)
    ]
    for turn, load in enumerate([basis_loads[0]] + loads + [basis_loads[1]]):
        load.start(priority=turn % 2)
    for load in loads:
        load.wait()

    keep = jnp.concatenate(
        [
            small_ref[w : w + 1, q * sub_rows : (q + 1) * sub_rows]
            for q in range(groups)
            for w in range(windows)
        ],
        axis=1,
    ).astype(jnp.float32)
    count = windows * channels

    def remote(peer):
        return pltpu.make_async_remote_copy(
            src_ref=send_v.at[peer], dst_ref=recv_v.at[me],
            send_sem=send_sem.at[peer], recv_sem=recv_sem.at[me],
            device_id={"rcv": peer}, device_id_type=pl.DeviceIdType.MESH,
        )

    def arrival(peer):
        return pltpu.make_async_remote_copy(
            src_ref=send_v.at[peer], dst_ref=recv_v.at[peer],
            send_sem=send_sem.at[peer], recv_sem=recv_sem.at[peer],
            device_id={"rcv": peer}, device_id_type=pl.DeviceIdType.MESH,
        )

    my_plane, my_place = me // pack, me % pack
    far_planes = [
        near_side * u + (1 - near_side) * (planes - 1 - u) for u in range(planes // 2)
    ]
    near_planes = [flipped(my_plane, u) for u in range(planes // 2 - 1, -1, -1)]
    for turn, side in enumerate(sides):
        basis_loads[turn].wait()
        halves = jnp.dot(
            rec_v[...].reshape(2 * count, half), basis_v[turn], preferred_element_type=jnp.float32
        )
        odd = lax.broadcasted_iota(jnp.int32, (count, halves.shape[1]), 1) % 2 == 1
        late = halves[count:]
        spectra = (halves[:count] + jnp.where(odd, -late, late)).T
        for b in range(NB // 2):
            spectrum = spectra[b * rows : (b + 1) * rows]
            power = jnp.sum(spectrum * spectrum, axis=0, keepdims=True) / BIN
            white = (spectrum * (keep * lax.rsqrt(power + 1e-05))).astype(jnp.bfloat16)
            for q in range(groups):
                send_v[side * (devices // 2) + b * groups + q] = white[:, q * LANES : (q + 1) * LANES]
        if turn == 0:
            pl.semaphore_wait(barrier, devices - 1)
        for plane in far_planes if turn == 0 else near_planes:
            own = turn == 1 and plane is near_planes[-1]
            for e in range(pack - 1, 0 if own else -1, -1):
                remote(plane * pack + flipped(my_place, e)).start()
    recv_v[me] = send_v[me]

    ordered = near_planes[::-1] + far_planes
    for turn, plane in enumerate(ordered):
        for e in range(0 if turn else 1, pack):
            arrival(plane * pack + flipped(my_place, e)).wait_recv()
        if turn == planes - 1:
            for s in range(NSB):
                own_v[s] = recv_v[small_ref[0, channels + s]]
            swap = pltpu.make_async_remote_copy(
                src_ref=own_v, dst_ref=src_ref.at[me % groups],
                send_sem=src_sem.at[0], recv_sem=src_sem.at[1],
                device_id={"rcv": flipped(me, 1)}, device_id_type=pl.DeviceIdType.MESH,
            )
            swap.start()
            src_ref[me % groups] = own_v[...]
        by_window = lanes_to_rows([recv_v[plane * pack + e] for e in range(pack)], sub_rows)
        for w, block in enumerate(by_window):
            real, imag = block[:BIN], block[BIN:]
            rhs_ref[0, plane, w * rows : w * rows + BIN] = real.astype(jnp.bfloat16)
            rhs_ref[0, plane, w * rows + BIN : (w + 1) * rows] = imag.astype(jnp.bfloat16)
            rhs_ref[1, plane, w * rows : w * rows + BIN] = imag.astype(jnp.bfloat16)
            rhs_ref[1, plane, w * rows + BIN : (w + 1) * rows] = (-real).astype(jnp.bfloat16)
    for off in range(1, devices):
        remote(flipped(me, off)).wait_send()
    swap.wait()


STEP_BINS = 4


def product_kernel(src_ref, rhs_ref, out_ref, left_v, out_v, out_sem):
    rows = 2 * BIN
    planes = rhs_ref.shape[1]
    windows = rhs_ref.shape[2] // rows
    groups, blocks = src_ref.shape[:2]
    sub_rows = SBLK // groups
    wide = 2

    pieces = [src_ref[q, s] for s in range(blocks) for q in range(groups)]
    by_window = lanes_to_rows(pieces, sub_rows)
    left_v[...] = jnp.concatenate(by_window, axis=0).T * (1.0 / windows)

    def write(place):
        return pltpu.make_async_copy(out_v.at[place], out_ref.at[place], out_sem.at[place])

    def step_body(step, carry):
        left = left_v[...]
        bin_of = lax.broadcasted_iota(jnp.int32, left.shape, 1) % BIN
        masked = jnp.concatenate(
            [
                jnp.where(bin_of == step * STEP_BINS + i, left, 0.0).astype(jnp.bfloat16)
                for i in range(STEP_BINS)
            ],
            axis=0,
        )
        for part in range(2):
            for z in range(0, planes, wide):
                right = jnp.concatenate([rhs_ref[part, z + u] for u in range(wide)], axis=1)
                both = jnp.dot(masked, right, preferred_element_type=jnp.float32)
                first = (part * planes + z) * LANES
                out_v[pl.ds(step * STEP_BINS, STEP_BINS), :, first : first + wide * LANES] = (
                    both.astype(jnp.bfloat16).reshape(STEP_BINS, left.shape[0], wide * LANES)
                )
        for i in range(STEP_BINS):
            write(step * STEP_BINS + i).start(priority=i % 2)
        return carry

    lax.fori_loop(0, BIN // STEP_BINS, step_body, 0)

    def wait_body(place, carry):
        write(place).wait()
        return carry

    lax.fori_loop(0, BIN, wait_body, 0)


def per_device_kernels(records, quality, block_ids):
    devices = lax.axis_size("rcv")
    groups = devices // NB
    windows, channels, samples = records.shape
    sub_rows = channels // groups
    pack = LANES // sub_rows
    planes = devices // pack
    rows = 2 * BIN
    depth = windows * rows
    table = basis_table(samples, samples // 2).reshape(samples // 2, 2, NB * BIN)
    basis = jnp.asarray(np.ascontiguousarray(table.transpose(1, 0, 2)))
    padded_ids = jnp.pad(block_ids.reshape(1, -1), ((0, windows - 1), (0, LANES - channels - NSB)))
    small = jnp.concatenate([quality, padded_ids], axis=1)
    rhs, src = pl.pallas_call(
        exchange_kernel,
        out_shape=(
            jax.ShapeDtypeStruct((2, planes, depth, LANES), jnp.bfloat16),
            jax.ShapeDtypeStruct((groups, NSB, rows, LANES), jnp.bfloat16),
        ),
        in_specs=[
            pl.BlockSpec(memory_space=pltpu.VMEM),
            pl.BlockSpec(memory_space=pltpu.HBM),
            pl.BlockSpec(memory_space=pltpu.HBM),
        ],
        out_specs=(pl.BlockSpec(memory_space=pltpu.VMEM), pl.BlockSpec(memory_space=pltpu.VMEM)),
        scratch_shapes=[
            pltpu.VMEM(basis.shape, jnp.bfloat16),
            pltpu.VMEM((2, windows * channels, samples // 2), jnp.bfloat16),
            pltpu.VMEM((devices, rows, LANES), jnp.bfloat16),
            pltpu.VMEM((devices, rows, LANES), jnp.bfloat16),
            pltpu.VMEM((NSB, rows, LANES), jnp.bfloat16),
            pltpu.SemaphoreType.DMA((2 * groups * windows,)),
            pltpu.SemaphoreType.DMA((2,)),
            pltpu.SemaphoreType.DMA((devices,)),
            pltpu.SemaphoreType.DMA((devices,)),
            pltpu.SemaphoreType.DMA((2,)),
        ],
        compiler_params=pltpu.CompilerParams(
            collective_id=0, has_side_effects=True, vmem_limit_bytes=53 * 2**20
        ),
        name="spectra_exchange",
    )(small, basis, records)

    count = NSB * SBLK
    out_shape = (BIN, count, 2 * planes * LANES)
    joined = pl.pallas_call(
        product_kernel,
        out_shape=jax.ShapeDtypeStruct(out_shape, jnp.bfloat16),
        in_specs=[pl.BlockSpec(memory_space=pltpu.VMEM)] * 2,
        out_specs=pl.BlockSpec(memory_space=pltpu.HBM),
        scratch_shapes=[
            pltpu.VMEM((count, depth), jnp.float32),
            pltpu.VMEM(out_shape, jnp.bfloat16),
            pltpu.SemaphoreType.DMA((BIN,)),
        ],
        compiler_params=pltpu.CompilerParams(vmem_limit_bytes=40 * 2**20),
        name="cross_spectra",
    )(src, rhs)
    return joined[None]


def make_basis(samples):
    return jnp.asarray(basis_table(samples, samples))


def from_partner(value, axis, stride):
    mask = 2**stride
    pairs = [(source, source ^ mask) for source in range(lax.axis_size(axis))]
    return lax.ppermute(value, axis, pairs)


def per_device_general(records, quality, block_ids):
    devices = lax.axis_size("rcv")
    groups = devices // NB
    windows, channels, samples = records.shape
    sub_rows = channels // groups
    basis_table = make_basis(samples).reshape(samples, NB, 2 * BIN)
    rec_rows = records.reshape(windows, groups, sub_rows, samples)
    spectrum = jnp.einsum(
        "wqjs,sbm->bqwjm", rec_rows, basis_table, preferred_element_type=jnp.float32
    )
    band_power = jnp.sum(spectrum * spectrum, axis=-1) / BIN
    keep_gate = quality.reshape(windows, groups, sub_rows).transpose(1, 0, 2).astype(jnp.float32)
    scaling = keep_gate[None] * lax.rsqrt(band_power + 1e-05)
    whitened = (spectrum * scaling[..., None]).astype(jnp.bfloat16)
    send_buf = whitened.reshape(devices, windows, sub_rows * 2 * BIN)
    arrived = lax.all_to_all(send_buf, "rcv", split_axis=0, concat_axis=0, tiled=True)
    receivers = arrived.reshape(devices, windows, sub_rows, 2, BIN)
    my_index = lax.axis_index("rcv")
    per_block = channels // SBLK
    blk_rows = SBLK // sub_rows
    own_pieces = []
    for source_slot in range(NSB):
        owner_dev = block_ids[source_slot] // per_block
        own_pieces.append(lax.dynamic_index_in_dim(arrived, owner_dev, 0, keepdims=False))
    collected = jnp.stack(own_pieces)[None]
    my_group = my_index % groups
    for bit_level in range(groups.bit_length() - 1):
        partner = from_partner(collected, "rcv", bit_level)
        upper_side = my_group // 2**bit_level % 2 == 1
        low_half = jnp.where(upper_side, partner, collected)
        high_half = jnp.where(upper_side, collected, partner)
        collected = jnp.concatenate([low_half, high_half], axis=0)
    slices = []
    for source_slot in range(NSB):
        slices.append(collected[:, source_slot])
    src_band = jnp.stack(slices).reshape(NSB, blk_rows, windows, sub_rows, 2, BIN)
    source_count = NSB * SBLK
    group_width = devices * sub_rows
    left_side = src_band.transpose(5, 0, 1, 3, 2, 4).reshape(BIN, source_count, windows, 2)
    rec_cols = receivers.transpose(4, 1, 3, 0, 2).reshape(BIN, windows, 2, group_width)
    rotated = jnp.stack([rec_cols[:, :, 1], -rec_cols[:, :, 0]], axis=2)
    right_side = jnp.concatenate([rec_cols, rotated], axis=-1)
    joined = jnp.einsum("inwp,iwpk->ink", left_side, right_side, preferred_element_type=jnp.float32)
    return (joined * (1.0 / windows)).astype(jnp.bfloat16)[None]


def per_device(records, quality, block_ids):
    devices = lax.axis_size("rcv")
    windows, channels, samples = records.shape
    groups = devices // NB
    sub_rows = channels // groups
    pack = LANES // sub_rows
    fits = (
        groups == 2
        and channels == SBLK
        and windows == pack
        and sub_rows * pack == LANES
        and NSB * groups == pack
        and devices % (2 * pack) == 0
        and FLO % 2 == 0
        and samples % 2 == 0
    )
    return (per_device_kernels if fits else per_device_general)(records, quality, block_ids)


def solution(mesh):
    placed = (P("grp", "rcv", None), P("grp", "rcv"), P("grp"))
    return jax.shard_map(
        per_device,
        mesh=mesh,
        in_specs=placed,
        out_specs=P("rcv", "grp", None, None),
        check_vma=False,
    )
```

```python
import functools

import jax
import jax.numpy as jnp
import ml_dtypes
import numpy as np
from jax import lax
from jax.experimental import pallas as pl
from jax.experimental.pallas import tpu as pltpu
from jax.sharding import PartitionSpec as P

NB = 8
BIN = 32
FLO = 64
SBLK = 64
NSB = 2
LANES = 128


def basis_table(samples, count):
    times = np.arange(count, dtype=np.int64)
    bins = FLO + np.arange(NB * BIN, dtype=np.int64)
    phases = (times[:, None] * bins[None, :]) % samples
    angles = phases.astype(np.float64) * (2.0 * np.pi / samples)
    table = np.stack([np.cos(angles), -np.sin(angles)]).reshape(2, count, NB, BIN)
    table = table.transpose(1, 2, 0, 3).reshape(count, NB * 2 * BIN)
    return table.astype(np.float32).astype(ml_dtypes.bfloat16)


def lanes_to_rows(pieces, width):
    lane = lax.broadcasted_iota(jnp.int32, pieces[0].shape, 1) // width
    wide = [piece.astype(jnp.float32) for piece in pieces]
    result = []
    for w in range(len(pieces)):
        total = None
        for e, piece in enumerate(wide):
            shift = (e - w) * width % LANES
            moved = pltpu.roll(piece, shift, 1) if shift else piece
            total = moved if total is None else jnp.where(lane == e, moved, total)
        result.append(total)
    return result


def flipped(me, off):
    other, bit = me, 1
    while bit <= off:
        if off & bit:
            other = other + bit * (1 - 2 * (me // bit % 2))
        bit *= 2
    return other


def exchange_kernel(
    small_ref, basis_ref, records_ref, rhs_ref, src_ref,
    basis_v, rec_v, send_v, recv_v, own_v,
    load_sem, basis_sem, send_sem, recv_sem, src_sem,
):
    devices = recv_v.shape[0]
    windows, channels, samples = records_ref.shape
    groups = devices // NB
    sub_rows = channels // groups
    pack = LANES // sub_rows
    planes = devices // pack
    half = samples // 2
    rows = 2 * BIN
    me = lax.axis_index("rcv")

    barrier = pltpu.get_barrier_semaphore()
    for off in range(1, devices):
        pl.semaphore_signal(
            barrier, inc=1, device_id={"rcv": flipped(me, off)},
            device_id_type=pl.DeviceIdType.MESH,
        )

    loads = []
    for q in range(groups):
        for w in range(windows):
            place = q * windows + w
            for h in range(2):
                loads.append(
                    pltpu.make_async_copy(
                        records_ref.at[w, pl.ds(q * sub_rows, sub_rows), pl.ds(h * half, half)],
                        rec_v.at[h, pl.ds(place * sub_rows, sub_rows)],
                        load_sem.at[2 * place + h],
                    )
                )
    near_side = me // (devices // 2)
    sides = (1 - near_side, near_side)
    basis_loads = [
        pltpu.make_async_copy(basis_ref.at[side], basis_v.at[turn], basis_sem.at[turn])
        for turn, side in enumerate(sides)
    ]
    for turn, load in enumerate([basis_loads[0]] + loads + [basis_loads[1]]):
        load.start(priority=turn % 2)
    for load in loads:
        load.wait()

    keep = jnp.concatenate(
        [
            small_ref[w : w + 1, q * sub_rows : (q + 1) * sub_rows]
            for q in range(groups)
            for w in range(windows)
        ],
        axis=1,
    ).astype(jnp.float32)
    count = windows * channels

    def remote(peer):
        return pltpu.make_async_remote_copy(
            src_ref=send_v.at[peer], dst_ref=recv_v.at[me],
            send_sem=send_sem.at[peer], recv_sem=recv_sem.at[me],
            device_id={"rcv": peer}, device_id_type=pl.DeviceIdType.MESH,
        )

    def arrival(peer):
        return pltpu.make_async_remote_copy(
            src_ref=send_v.at[peer], dst_ref=recv_v.at[peer],
            send_sem=send_sem.at[peer], recv_sem=recv_sem.at[peer],
            device_id={"rcv": peer}, device_id_type=pl.DeviceIdType.MESH,
        )

    my_plane, my_place = me // pack, me % pack
    far_planes = [
        near_side * u + (1 - near_side) * (planes - 1 - u) for u in range(planes // 2)
    ]
    near_planes = [flipped(my_plane, u) for u in range(planes // 2 - 1, -1, -1)]
    for turn, side in enumerate(sides):
        basis_loads[turn].wait()
        halves = jnp.dot(
            rec_v[...].reshape(2 * count, half), basis_v[turn], preferred_element_type=jnp.float32
        )
        odd = lax.broadcasted_iota(jnp.int32, (count, halves.shape[1]), 1) % 2 == 1
        late = halves[count:]
        spectra = (halves[:count] + jnp.where(odd, -late, late)).T
        for b in range(NB // 2):
            spectrum = spectra[b * rows : (b + 1) * rows]
            power = jnp.sum(spectrum * spectrum, axis=0, keepdims=True) / BIN
            white = (spectrum * (keep * lax.rsqrt(power + 1e-05))).astype(jnp.bfloat16)
            for q in range(groups):
                send_v[side * (devices // 2) + b * groups + q] = white[:, q * LANES : (q + 1) * LANES]
        if turn == 0:
            pl.semaphore_wait(barrier, devices - 1)
        for plane in far_planes if turn == 0 else near_planes:
            own = turn == 1 and plane is near_planes[-1]
            for e in range(pack - 1, 0 if own else -1, -1):
                remote(plane * pack + flipped(my_place, e)).start()
    recv_v[me] = send_v[me]

    ordered = near_planes[::-1] + far_planes
    for turn, plane in enumerate(ordered):
        for e in range(0 if turn else 1, pack):
            arrival(plane * pack + flipped(my_place, e)).wait_recv()
        if turn == planes - 1:
            for s in range(NSB):
                own_v[s] = recv_v[small_ref[0, channels + s]]
            swap = pltpu.make_async_remote_copy(
                src_ref=own_v, dst_ref=src_ref.at[me % groups],
                send_sem=src_sem.at[0], recv_sem=src_sem.at[1],
                device_id={"rcv": flipped(me, 1)}, device_id_type=pl.DeviceIdType.MESH,
            )
            swap.start()
            src_ref[me % groups] = own_v[...]
        by_window = lanes_to_rows([recv_v[plane * pack + e] for e in range(pack)], sub_rows)
        for w, block in enumerate(by_window):
            real, imag = block[:BIN], block[BIN:]
            rhs_ref[0, plane, w * rows : w * rows + BIN] = real.astype(jnp.bfloat16)
            rhs_ref[0, plane, w * rows + BIN : (w + 1) * rows] = imag.astype(jnp.bfloat16)
            rhs_ref[1, plane, w * rows : w * rows + BIN] = imag.astype(jnp.bfloat16)
            rhs_ref[1, plane, w * rows + BIN : (w + 1) * rows] = (-real).astype(jnp.bfloat16)
    for off in range(1, devices):
        remote(flipped(me, off)).wait_send()
    swap.wait()


STEP_BINS = 4


def product_kernel(src_ref, rhs_ref, out_ref, left_v, out_v, out_sem):
    rows = 2 * BIN
    planes = rhs_ref.shape[1]
    windows = rhs_ref.shape[2] // rows
    groups, blocks = src_ref.shape[:2]
    sub_rows = SBLK // groups
    wide = 2

    pieces = [src_ref[q, s] for s in range(blocks) for q in range(groups)]
    by_window = lanes_to_rows(pieces, sub_rows)
    left_v[...] = jnp.concatenate(by_window, axis=0).T * (1.0 / windows)

    def write(place):
        return pltpu.make_async_copy(out_v.at[place], out_ref.at[place], out_sem.at[place])

    for step in range(BIN // STEP_BINS):
        left = left_v[...]
        bin_of = lax.broadcasted_iota(jnp.int32, left.shape, 1) % BIN
        masked = jnp.concatenate(
            [
                jnp.where(bin_of == step * STEP_BINS + i, left, 0.0).astype(jnp.bfloat16)
                for i in range(STEP_BINS)
            ],
            axis=0,
        )
        for part in range(2):
            for z in range(0, planes, wide):
                right = jnp.concatenate([rhs_ref[part, z + u] for u in range(wide)], axis=1)
                both = jnp.dot(masked, right, preferred_element_type=jnp.float32)
                first = (part * planes + z) * LANES
                out_v[pl.ds(step * STEP_BINS, STEP_BINS), :, first : first + wide * LANES] = (
                    both.astype(jnp.bfloat16).reshape(STEP_BINS, left.shape[0], wide * LANES)
                )
        for i in range(STEP_BINS):
            write(step * STEP_BINS + i).start(priority=i % 2)

    def wait_body(place, carry):
        write(place).wait()
        return carry

    lax.fori_loop(0, BIN, wait_body, 0)


def per_device_kernels(records, quality, block_ids):
    devices = lax.axis_size("rcv")
    groups = devices // NB
    windows, channels, samples = records.shape
    sub_rows = channels // groups
    pack = LANES // sub_rows
    planes = devices // pack
    rows = 2 * BIN
    depth = windows * rows
    table = basis_table(samples, samples // 2).reshape(samples // 2, 2, NB * BIN)
    basis = jnp.asarray(np.ascontiguousarray(table.transpose(1, 0, 2)))
    padded_ids = jnp.pad(block_ids.reshape(1, -1), ((0, windows - 1), (0, LANES - channels - NSB)))
    small = jnp.concatenate([quality, padded_ids], axis=1)
    rhs, src = pl.pallas_call(
        exchange_kernel,
        out_shape=(
            jax.ShapeDtypeStruct((2, planes, depth, LANES), jnp.bfloat16),
            jax.ShapeDtypeStruct((groups, NSB, rows, LANES), jnp.bfloat16),
        ),
        in_specs=[
            pl.BlockSpec(memory_space=pltpu.VMEM),
            pl.BlockSpec(memory_space=pltpu.HBM),
            pl.BlockSpec(memory_space=pltpu.HBM),
        ],
        out_specs=(pl.BlockSpec(memory_space=pltpu.VMEM), pl.BlockSpec(memory_space=pltpu.VMEM)),
        scratch_shapes=[
            pltpu.VMEM(basis.shape, jnp.bfloat16),
            pltpu.VMEM((2, windows * channels, samples // 2), jnp.bfloat16),
            pltpu.VMEM((devices, rows, LANES), jnp.bfloat16),
            pltpu.VMEM((devices, rows, LANES), jnp.bfloat16),
            pltpu.VMEM((NSB, rows, LANES), jnp.bfloat16),
            pltpu.SemaphoreType.DMA((2 * groups * windows,)),
            pltpu.SemaphoreType.DMA((2,)),
            pltpu.SemaphoreType.DMA((devices,)),
            pltpu.SemaphoreType.DMA((devices,)),
            pltpu.SemaphoreType.DMA((2,)),
        ],
        compiler_params=pltpu.CompilerParams(
            collective_id=0, has_side_effects=True, vmem_limit_bytes=53 * 2**20
        ),
        name="spectra_exchange",
    )(small, basis, records)

    count = NSB * SBLK
    out_shape = (BIN, count, 2 * planes * LANES)
    joined = pl.pallas_call(
        product_kernel,
        out_shape=jax.ShapeDtypeStruct(out_shape, jnp.bfloat16),
        in_specs=[pl.BlockSpec(memory_space=pltpu.VMEM)] * 2,
        out_specs=pl.BlockSpec(memory_space=pltpu.HBM),
        scratch_shapes=[
            pltpu.VMEM((count, depth), jnp.float32),
            pltpu.VMEM(out_shape, jnp.bfloat16),
            pltpu.SemaphoreType.DMA((BIN,)),
        ],
        compiler_params=pltpu.CompilerParams(vmem_limit_bytes=40 * 2**20),
        name="cross_spectra",
    )(src, rhs)
    return joined[None]


def make_basis(samples):
    return jnp.asarray(basis_table(samples, samples))


def from_partner(value, axis, stride):
    mask = 2**stride
    pairs = [(source, source ^ mask) for source in range(lax.axis_size(axis))]
    return lax.ppermute(value, axis, pairs)


def per_device_general(records, quality, block_ids):
    devices = lax.axis_size("rcv")
    groups = devices // NB
    windows, channels, samples = records.shape
    sub_rows = channels // groups
    basis_table = make_basis(samples).reshape(samples, NB, 2 * BIN)
    rec_rows = records.reshape(windows, groups, sub_rows, samples)
    spectrum = jnp.einsum(
        "wqjs,sbm->bqwjm", rec_rows, basis_table, preferred_element_type=jnp.float32
    )
    band_power = jnp.sum(spectrum * spectrum, axis=-1) / BIN
    keep_gate = quality.reshape(windows, groups, sub_rows).transpose(1, 0, 2).astype(jnp.float32)
    scaling = keep_gate[None] * lax.rsqrt(band_power + 1e-05)
    whitened = (spectrum * scaling[..., None]).astype(jnp.bfloat16)
    send_buf = whitened.reshape(devices, windows, sub_rows * 2 * BIN)
    arrived = lax.all_to_all(send_buf, "rcv", split_axis=0, concat_axis=0, tiled=True)
    receivers = arrived.reshape(devices, windows, sub_rows, 2, BIN)
    my_index = lax.axis_index("rcv")
    per_block = channels // SBLK
    blk_rows = SBLK // sub_rows
    own_pieces = []
    for source_slot in range(NSB):
        owner_dev = block_ids[source_slot] // per_block
        own_pieces.append(lax.dynamic_index_in_dim(arrived, owner_dev, 0, keepdims=False))
    collected = jnp.stack(own_pieces)[None]
    my_group = my_index % groups
    for bit_level in range(groups.bit_length() - 1):
        partner = from_partner(collected, "rcv", bit_level)
        upper_side = my_group // 2**bit_level % 2 == 1
        low_half = jnp.where(upper_side, partner, collected)
        high_half = jnp.where(upper_side, collected, partner)
        collected = jnp.concatenate([low_half, high_half], axis=0)
    slices = []
    for source_slot in range(NSB):
        slices.append(collected[:, source_slot])
    src_band = jnp.stack(slices).reshape(NSB, blk_rows, windows, sub_rows, 2, BIN)
    source_count = NSB * SBLK
    group_width = devices * sub_rows
    left_side = src_band.transpose(5, 0, 1, 3, 2, 4).reshape(BIN, source_count, windows, 2)
    rec_cols = receivers.transpose(4, 1, 3, 0, 2).reshape(BIN, windows, 2, group_width)
    rotated = jnp.stack([rec_cols[:, :, 1], -rec_cols[:, :, 0]], axis=2)
    right_side = jnp.concatenate([rec_cols, rotated], axis=-1)
    joined = jnp.einsum("inwp,iwpk->ink", left_side, right_side, preferred_element_type=jnp.float32)
    return (joined * (1.0 / windows)).astype(jnp.bfloat16)[None]


def per_device(records, quality, block_ids):
    devices = lax.axis_size("rcv")
    windows, channels, samples = records.shape
    groups = devices // NB
    sub_rows = channels // groups
    pack = LANES // sub_rows
    fits = (
        groups == 2
        and channels == SBLK
        and windows == pack
        and sub_rows * pack == LANES
        and NSB * groups == pack
        and devices % (2 * pack) == 0
        and FLO % 2 == 0
        and samples % 2 == 0
    )
    return (per_device_kernels if fits else per_device_general)(records, quality, block_ids)


def solution(mesh):
    placed = (P("grp", "rcv", None), P("grp", "rcv"), P("grp"))
    return jax.shard_map(
        per_device,
        mesh=mesh,
        in_specs=placed,
        out_specs=P("rcv", "grp", None, None),
        check_vma=False,
    )
```

```python
import functools

import jax
import jax.numpy as jnp
import ml_dtypes
import numpy as np
from jax import lax
from jax.experimental import pallas as pl
from jax.experimental.pallas import tpu as pltpu
from jax.sharding import PartitionSpec as P

NB = 8
BIN = 32
FLO = 64
SBLK = 64
NSB = 2
LANES = 128
TIME_BLOCKS = 2


def basis_table(samples, count):
    times = np.arange(count, dtype=np.int64)
    bins = FLO + np.arange(NB * BIN, dtype=np.int64)
    phases = (times[:, None] * bins[None, :]) % samples
    angles = phases.astype(np.float64) * (2.0 * np.pi / samples)
    table = np.stack([np.cos(angles), -np.sin(angles)]).reshape(2, count, NB, BIN)
    table = table.transpose(1, 2, 0, 3).reshape(count, NB * 2 * BIN)
    return table.astype(np.float32).astype(ml_dtypes.bfloat16)


def lanes_to_rows(pieces, width):
    lane = lax.broadcasted_iota(jnp.int32, pieces[0].shape, 1) // width
    wide = [piece.astype(jnp.float32) for piece in pieces]
    result = []
    for w in range(len(pieces)):
        total = None
        for e, piece in enumerate(wide):
            shift = (e - w) * width % LANES
            moved = pltpu.roll(piece, shift, 1) if shift else piece
            total = moved if total is None else jnp.where(lane == e, moved, total)
        result.append(total)
    return result


def flipped(me, off):
    other, bit = me, 1
    while bit <= off:
        if off & bit:
            other = other + bit * (1 - 2 * (me // bit % 2))
        bit *= 2
    return other


def exchange_kernel(
    small_ref, basis_ref, records_ref, rhs_ref, src_ref,
    basis_v, rec_v, send_v, recv_v, own_v,
    load_sem, basis_sem, send_sem, recv_sem, src_sem,
):
    devices = recv_v.shape[0]
    windows, channels, samples = records_ref.shape
    groups = devices // NB
    sub_rows = channels // groups
    pack = LANES // sub_rows
    planes = devices // pack
    half = samples // 2
    rows = 2 * BIN
    me = lax.axis_index("rcv")

    barrier = pltpu.get_barrier_semaphore()
    for off in range(1, devices):
        pl.semaphore_signal(
            barrier, inc=1, device_id={"rcv": flipped(me, off)},
            device_id_type=pl.DeviceIdType.MESH,
        )

    near_side = me // (devices // 2)
    sides = (1 - near_side, near_side)
    part = half // TIME_BLOCKS

    def basis_load(turn, block):
        piece = pl.ds(block * part, part)
        return pltpu.make_async_copy(
            basis_ref.at[sides[turn], piece], basis_v.at[turn, piece], basis_sem.at[turn, block]
        )

    def record_loads(block):
        result = []
        for q in range(groups):
            for w in range(windows):
                place = q * windows + w
                for h in range(2):
                    result.append(
                        pltpu.make_async_copy(
                            records_ref.at[
                                w, pl.ds(q * sub_rows, sub_rows), pl.ds(h * half + block * part, part)
                            ],
                            rec_v.at[block, h, pl.ds(place * sub_rows, sub_rows)],
                            load_sem.at[block, 2 * place + h],
                        )
                    )
        return result

    for block in range(TIME_BLOCKS):
        basis_load(0, block).start()
        for turn, load in enumerate(record_loads(block)):
            load.start(priority=turn % 2)
    for block in range(TIME_BLOCKS):
        basis_load(1, block).start()

    count = windows * channels

    def remote(peer):
        return pltpu.make_async_remote_copy(
            src_ref=send_v.at[peer], dst_ref=recv_v.at[me],
            send_sem=send_sem.at[peer], recv_sem=recv_sem.at[me],
            device_id={"rcv": peer}, device_id_type=pl.DeviceIdType.MESH,
        )

    def arrival(peer):
        return pltpu.make_async_remote_copy(
            src_ref=send_v.at[peer], dst_ref=recv_v.at[peer],
            send_sem=send_sem.at[peer], recv_sem=recv_sem.at[peer],
            device_id={"rcv": peer}, device_id_type=pl.DeviceIdType.MESH,
        )

    my_plane, my_place = me // pack, me % pack
    far_planes = [
        near_side * u + (1 - near_side) * (planes - 1 - u) for u in range(planes // 2)
    ]
    near_planes = [flipped(my_plane, u) for u in range(planes // 2 - 1, -1, -1)]
    for turn, side in enumerate(sides):
        halves = 0.0
        for block in range(TIME_BLOCKS):
            basis_load(turn, block).wait()
            if turn == 0:
                for load in record_loads(block):
                    load.wait()
            halves = halves + jnp.dot(
                rec_v[block].reshape(2 * count, part),
                basis_v[turn, block * part : (block + 1) * part],
                preferred_element_type=jnp.float32,
            )
        if turn == 0:
            keep = jnp.concatenate(
                [
                    small_ref[w : w + 1, q * sub_rows : (q + 1) * sub_rows]
                    for q in range(groups)
                    for w in range(windows)
                ],
                axis=1,
            ).astype(jnp.float32)
        odd = lax.broadcasted_iota(jnp.int32, (count, halves.shape[1]), 1) % 2 == 1
        late = halves[count:]
        spectra = (halves[:count] + jnp.where(odd, -late, late)).T
        for b in range(NB // 2):
            spectrum = spectra[b * rows : (b + 1) * rows]
            power = jnp.sum(spectrum * spectrum, axis=0, keepdims=True) / BIN
            white = (spectrum * (keep * lax.rsqrt(power + 1e-05))).astype(jnp.bfloat16)
            for q in range(groups):
                send_v[side * (devices // 2) + b * groups + q] = white[:, q * LANES : (q + 1) * LANES]
        if turn == 0:
            pl.semaphore_wait(barrier, devices - 1)
        for plane in far_planes if turn == 0 else near_planes:
            own = turn == 1 and plane is near_planes[-1]
            for e in range(pack - 1, 0 if own else -1, -1):
                remote(plane * pack + flipped(my_place, e)).start()
    recv_v[me] = send_v[me]

    ordered = near_planes[::-1] + far_planes
    for turn, plane in enumerate(ordered):
        for e in range(0 if turn else 1, pack):
            arrival(plane * pack + flipped(my_place, e)).wait_recv()
        if turn == planes - 1:
            for s in range(NSB):
                own_v[s] = recv_v[small_ref[0, channels + s]]
            swap = pltpu.make_async_remote_copy(
                src_ref=own_v, dst_ref=src_ref.at[me % groups],
                send_sem=src_sem.at[0], recv_sem=src_sem.at[1],
                device_id={"rcv": flipped(me, 1)}, device_id_type=pl.DeviceIdType.MESH,
            )
            swap.start()
            src_ref[me % groups] = own_v[...]
        by_window = lanes_to_rows([recv_v[plane * pack + e] for e in range(pack)], sub_rows)
        for w, block in enumerate(by_window):
            real, imag = block[:BIN], block[BIN:]
            rhs_ref[0, plane, w * rows : w * rows + BIN] = real.astype(jnp.bfloat16)
            rhs_ref[0, plane, w * rows + BIN : (w + 1) * rows] = imag.astype(jnp.bfloat16)
            rhs_ref[1, plane, w * rows : w * rows + BIN] = imag.astype(jnp.bfloat16)
            rhs_ref[1, plane, w * rows + BIN : (w + 1) * rows] = (-real).astype(jnp.bfloat16)
    for off in range(1, devices):
        remote(flipped(me, off)).wait_send()
    swap.wait()


def bin_steps():
    first, steps = 0, []
    while first < BIN:
        width = min(8, max(2, first), BIN - first)
        steps.append((first, width))
        first += width
    return steps


def product_kernel(src_ref, rhs_ref, out_ref, left_v, out_v, out_sem):
    rows = 2 * BIN
    planes = rhs_ref.shape[1]
    windows = rhs_ref.shape[2] // rows
    groups, blocks = src_ref.shape[:2]
    sub_rows = SBLK // groups
    wide = 2

    pieces = [src_ref[q, s] for s in range(blocks) for q in range(groups)]
    by_window = lanes_to_rows(pieces, sub_rows)
    left_v[...] = jnp.concatenate(by_window, axis=0).T * (1.0 / windows)

    def write(place):
        return pltpu.make_async_copy(out_v.at[place], out_ref.at[place], out_sem.at[place])

    for begin, bins in bin_steps():
        left = left_v[...]
        bin_of = lax.broadcasted_iota(jnp.int32, left.shape, 1) % BIN
        masked = jnp.concatenate(
            [
                jnp.where(bin_of == begin + i, left, 0.0).astype(jnp.bfloat16)
                for i in range(bins)
            ],
            axis=0,
        )
        for part in range(2):
            for z in range(0, planes, wide):
                right = jnp.concatenate([rhs_ref[part, z + u] for u in range(wide)], axis=1)
                both = jnp.dot(masked, right, preferred_element_type=jnp.float32)
                first = (part * planes + z) * LANES
                out_v[begin : begin + bins, :, first : first + wide * LANES] = (
                    both.astype(jnp.bfloat16).reshape(bins, left.shape[0], wide * LANES)
                )
        for i in range(bins):
            write(begin + i).start(priority=i % 2)

    def wait_body(place, carry):
        write(place).wait()
        return carry

    lax.fori_loop(0, BIN, wait_body, 0)


def per_device_kernels(records, quality, block_ids):
    devices = lax.axis_size("rcv")
    groups = devices // NB
    windows, channels, samples = records.shape
    sub_rows = channels // groups
    pack = LANES // sub_rows
    planes = devices // pack
    rows = 2 * BIN
    depth = windows * rows
    table = basis_table(samples, samples // 2).reshape(samples // 2, 2, NB * BIN)
    basis = jnp.asarray(np.ascontiguousarray(table.transpose(1, 0, 2)))
    padded_ids = jnp.pad(block_ids.reshape(1, -1), ((0, windows - 1), (0, LANES - channels - NSB)))
    small = jnp.concatenate([quality, padded_ids], axis=1)
    rhs, src = pl.pallas_call(
        exchange_kernel,
        out_shape=(
            jax.ShapeDtypeStruct((2, planes, depth, LANES), jnp.bfloat16),
            jax.ShapeDtypeStruct((groups, NSB, rows, LANES), jnp.bfloat16),
        ),
        in_specs=[
            pl.BlockSpec(memory_space=pltpu.VMEM),
            pl.BlockSpec(memory_space=pltpu.HBM),
            pl.BlockSpec(memory_space=pltpu.HBM),
        ],
        out_specs=(pl.BlockSpec(memory_space=pltpu.VMEM), pl.BlockSpec(memory_space=pltpu.VMEM)),
        scratch_shapes=[
            pltpu.VMEM(basis.shape, jnp.bfloat16),
            pltpu.VMEM(
                (TIME_BLOCKS, 2, windows * channels, samples // 2 // TIME_BLOCKS), jnp.bfloat16
            ),
            pltpu.VMEM((devices, rows, LANES), jnp.bfloat16),
            pltpu.VMEM((devices, rows, LANES), jnp.bfloat16),
            pltpu.VMEM((NSB, rows, LANES), jnp.bfloat16),
            pltpu.SemaphoreType.DMA((TIME_BLOCKS, 2 * groups * windows)),
            pltpu.SemaphoreType.DMA((2, TIME_BLOCKS)),
            pltpu.SemaphoreType.DMA((devices,)),
            pltpu.SemaphoreType.DMA((devices,)),
            pltpu.SemaphoreType.DMA((2,)),
        ],
        compiler_params=pltpu.CompilerParams(
            collective_id=0, has_side_effects=True, vmem_limit_bytes=53 * 2**20
        ),
        name="spectra_exchange",
    )(small, basis, records)

    count = NSB * SBLK
    out_shape = (BIN, count, 2 * planes * LANES)
    joined = pl.pallas_call(
        product_kernel,
        out_shape=jax.ShapeDtypeStruct(out_shape, jnp.bfloat16),
        in_specs=[pl.BlockSpec(memory_space=pltpu.VMEM)] * 2,
        out_specs=pl.BlockSpec(memory_space=pltpu.HBM),
        scratch_shapes=[
            pltpu.VMEM((count, depth), jnp.float32),
            pltpu.VMEM(out_shape, jnp.bfloat16),
            pltpu.SemaphoreType.DMA((BIN,)),
        ],
        compiler_params=pltpu.CompilerParams(vmem_limit_bytes=40 * 2**20),
        name="cross_spectra",
    )(src, rhs)
    return joined[None]


def make_basis(samples):
    return jnp.asarray(basis_table(samples, samples))


def from_partner(value, axis, stride):
    mask = 2**stride
    pairs = [(source, source ^ mask) for source in range(lax.axis_size(axis))]
    return lax.ppermute(value, axis, pairs)


def per_device_general(records, quality, block_ids):
    devices = lax.axis_size("rcv")
    groups = devices // NB
    windows, channels, samples = records.shape
    sub_rows = channels // groups
    basis_table = make_basis(samples).reshape(samples, NB, 2 * BIN)
    rec_rows = records.reshape(windows, groups, sub_rows, samples)
    spectrum = jnp.einsum(
        "wqjs,sbm->bqwjm", rec_rows, basis_table, preferred_element_type=jnp.float32
    )
    band_power = jnp.sum(spectrum * spectrum, axis=-1) / BIN
    keep_gate = quality.reshape(windows, groups, sub_rows).transpose(1, 0, 2).astype(jnp.float32)
    scaling = keep_gate[None] * lax.rsqrt(band_power + 1e-05)
    whitened = (spectrum * scaling[..., None]).astype(jnp.bfloat16)
    send_buf = whitened.reshape(devices, windows, sub_rows * 2 * BIN)
    arrived = lax.all_to_all(send_buf, "rcv", split_axis=0, concat_axis=0, tiled=True)
    receivers = arrived.reshape(devices, windows, sub_rows, 2, BIN)
    my_index = lax.axis_index("rcv")
    per_block = channels // SBLK
    blk_rows = SBLK // sub_rows
    own_pieces = []
    for source_slot in range(NSB):
        owner_dev = block_ids[source_slot] // per_block
        own_pieces.append(lax.dynamic_index_in_dim(arrived, owner_dev, 0, keepdims=False))
    collected = jnp.stack(own_pieces)[None]
    my_group = my_index % groups
    for bit_level in range(groups.bit_length() - 1):
        partner = from_partner(collected, "rcv", bit_level)
        upper_side = my_group // 2**bit_level % 2 == 1
        low_half = jnp.where(upper_side, partner, collected)
        high_half = jnp.where(upper_side, collected, partner)
        collected = jnp.concatenate([low_half, high_half], axis=0)
    slices = []
    for source_slot in range(NSB):
        slices.append(collected[:, source_slot])
    src_band = jnp.stack(slices).reshape(NSB, blk_rows, windows, sub_rows, 2, BIN)
    source_count = NSB * SBLK
    group_width = devices * sub_rows
    left_side = src_band.transpose(5, 0, 1, 3, 2, 4).reshape(BIN, source_count, windows, 2)
    rec_cols = receivers.transpose(4, 1, 3, 0, 2).reshape(BIN, windows, 2, group_width)
    rotated = jnp.stack([rec_cols[:, :, 1], -rec_cols[:, :, 0]], axis=2)
    right_side = jnp.concatenate([rec_cols, rotated], axis=-1)
    joined = jnp.einsum("inwp,iwpk->ink", left_side, right_side, preferred_element_type=jnp.float32)
    return (joined * (1.0 / windows)).astype(jnp.bfloat16)[None]


def per_device(records, quality, block_ids):
    devices = lax.axis_size("rcv")
    windows, channels, samples = records.shape
    groups = devices // NB
    sub_rows = channels // groups
    pack = LANES // sub_rows
    fits = (
        groups == 2
        and channels == SBLK
        and windows == pack
        and sub_rows * pack == LANES
        and NSB * groups == pack
        and devices % (2 * pack) == 0
        and FLO % 2 == 0
        and samples % 2 == 0
    )
    return (per_device_kernels if fits else per_device_general)(records, quality, block_ids)


def solution(mesh):
    placed = (P("grp", "rcv", None), P("grp", "rcv"), P("grp"))
    return jax.shard_map(
        per_device,
        mesh=mesh,
        in_specs=placed,
        out_specs=P("rcv", "grp", None, None),
        check_vma=False,
    )
```

```python
import functools

import jax
import jax.numpy as jnp
import ml_dtypes
import numpy as np
from jax import lax
from jax.experimental import pallas as pl
from jax.experimental.pallas import tpu as pltpu
from jax.sharding import PartitionSpec as P

NB = 8
BIN = 32
FLO = 64
SBLK = 64
NSB = 2
LANES = 128


def basis_table(samples, count):
    times = np.arange(count, dtype=np.int64)
    bins = FLO + np.arange(NB * BIN, dtype=np.int64)
    phases = (times[:, None] * bins[None, :]) % samples
    angles = phases.astype(np.float64) * (2.0 * np.pi / samples)
    table = np.stack([np.cos(angles), -np.sin(angles)]).reshape(2, count, NB, BIN)
    table = table.transpose(1, 2, 0, 3).reshape(count, NB * 2 * BIN)
    return table.astype(np.float32).astype(ml_dtypes.bfloat16)


def lanes_to_rows(pieces, width):
    lane = lax.broadcasted_iota(jnp.int32, pieces[0].shape, 1) // width
    wide = [piece.astype(jnp.float32) for piece in pieces]
    result = []
    for w in range(len(pieces)):
        total = None
        for e, piece in enumerate(wide):
            shift = (e - w) * width % LANES
            moved = pltpu.roll(piece, shift, 1) if shift else piece
            total = moved if total is None else jnp.where(lane == e, moved, total)
        result.append(total)
    return result


def flipped(me, off):
    other, bit = me, 1
    while bit <= off:
        if off & bit:
            other = other + bit * (1 - 2 * (me // bit % 2))
        bit *= 2
    return other


def exchange_kernel(
    small_ref, basis_ref, records_ref, rhs_ref, src_ref,
    basis_v, rec_v, send_v, recv_v, own_v,
    load_sem, basis_sem, send_sem, recv_sem, src_sem,
):
    devices = recv_v.shape[0]
    windows, channels, samples = records_ref.shape
    groups = devices // NB
    sub_rows = channels // groups
    pack = LANES // sub_rows
    planes = devices // pack
    half = samples // 2
    rows = 2 * BIN
    me = lax.axis_index("rcv")

    barrier = pltpu.get_barrier_semaphore()
    for off in range(1, devices):
        pl.semaphore_signal(
            barrier, inc=1, device_id={"rcv": flipped(me, off)},
            device_id_type=pl.DeviceIdType.MESH,
        )

    near_side = me // (devices // 2)
    sides = (1 - near_side, near_side)
    basis_loads = [
        pltpu.make_async_copy(basis_ref.at[side], basis_v.at[turn], basis_sem.at[turn])
        for turn, side in enumerate(sides)
    ]
    loads = []
    for q in range(groups):
        loads.append([])
        for w in range(windows):
            for h in range(2):
                loads[q].append(
                    pltpu.make_async_copy(
                        records_ref.at[w, pl.ds(q * sub_rows, sub_rows), pl.ds(h * half, half)],
                        rec_v.at[q, h, pl.ds(w * sub_rows, sub_rows)],
                        load_sem.at[q, 2 * w + h],
                    )
                )
    basis_loads[0].start()
    for group_loads in loads:
        for turn, load in enumerate(group_loads):
            load.start(priority=turn % 2)
    basis_loads[1].start()

    def remote(peer):
        return pltpu.make_async_remote_copy(
            src_ref=send_v.at[peer], dst_ref=recv_v.at[me],
            send_sem=send_sem.at[peer], recv_sem=recv_sem.at[me],
            device_id={"rcv": peer}, device_id_type=pl.DeviceIdType.MESH,
        )

    def arrival(peer):
        return pltpu.make_async_remote_copy(
            src_ref=send_v.at[peer], dst_ref=recv_v.at[peer],
            send_sem=send_sem.at[peer], recv_sem=recv_sem.at[peer],
            device_id={"rcv": peer}, device_id_type=pl.DeviceIdType.MESH,
        )

    my_plane, my_place = me // pack, me % pack
    far_planes = [
        near_side * u + (1 - near_side) * (planes - 1 - u) for u in range(planes // 2)
    ]
    near_planes = [flipped(my_plane, u) for u in range(planes // 2 - 1, -1, -1)]
    odd = lax.broadcasted_iota(jnp.int32, (LANES, NB * BIN), 1) % 2 == 1
    for turn, side in enumerate(sides):
        basis_loads[turn].wait()
        for q in range(groups):
            if turn == 0:
                for load in loads[q]:
                    load.wait()
            keep = jnp.concatenate(
                [small_ref[w : w + 1, q * sub_rows : (q + 1) * sub_rows] for w in range(windows)],
                axis=1,
            ).astype(jnp.float32)
            halves = jnp.dot(
                rec_v[q].reshape(2 * LANES, half), basis_v[turn], preferred_element_type=jnp.float32
            )
            late = halves[LANES:]
            spectra = (halves[:LANES] + jnp.where(odd, -late, late)).T
            for b in range(NB // 2):
                spectrum = spectra[b * rows : (b + 1) * rows]
                power = jnp.sum(spectrum * spectrum, axis=0, keepdims=True) / BIN
                white = spectrum * (keep * lax.rsqrt(power + 1e-05))
                send_v[side * (devices // 2) + b * groups + q] = white.astype(jnp.bfloat16)
            if turn == 0 and q == 0:
                pl.semaphore_wait(barrier, devices - 1)
            for plane in far_planes if turn == 0 else near_planes:
                for v in range(pack // groups - 1, -1, -1):
                    peer = plane * pack + flipped(my_place // groups, v) * groups + q
                    if turn == 1 and plane is near_planes[-1] and v == 0:
                        pl.when(me % groups != q)(remote(peer).start)
                    else:
                        remote(peer).start()
    recv_v[me] = send_v[me]

    ordered = near_planes[::-1] + far_planes
    for turn, plane in enumerate(ordered):
        for e in range(0 if turn else 1, pack):
            arrival(plane * pack + flipped(my_place, e)).wait_recv()
        if turn == planes - 1:
            for s in range(NSB):
                turned = recv_v[small_ref[0, channels + s]].astype(jnp.float32).T * (1.0 / windows)
                own_v[s] = jnp.concatenate(
                    [turned[w * sub_rows : (w + 1) * sub_rows] for w in range(windows)], axis=1
                ).astype(jnp.bfloat16)
            swap = pltpu.make_async_remote_copy(
                src_ref=own_v, dst_ref=src_ref.at[me % groups],
                send_sem=src_sem.at[0], recv_sem=src_sem.at[1],
                device_id={"rcv": flipped(me, 1)}, device_id_type=pl.DeviceIdType.MESH,
            )
            swap.start()
            src_ref[me % groups] = own_v[...]
        by_window = lanes_to_rows([recv_v[plane * pack + e] for e in range(pack)], sub_rows)
        for w, block in enumerate(by_window):
            real, imag = block[:BIN], block[BIN:]
            rhs_ref[0, plane, w * rows : w * rows + BIN] = real.astype(jnp.bfloat16)
            rhs_ref[0, plane, w * rows + BIN : (w + 1) * rows] = imag.astype(jnp.bfloat16)
            rhs_ref[1, plane, w * rows : w * rows + BIN] = imag.astype(jnp.bfloat16)
            rhs_ref[1, plane, w * rows + BIN : (w + 1) * rows] = (-real).astype(jnp.bfloat16)
    for off in range(1, devices):
        remote(flipped(me, off)).wait_send()
    swap.wait()


STEP_BINS = 4


def product_kernel(src_ref, rhs_ref, out_ref, left_v, out_v, out_sem):
    planes = rhs_ref.shape[1]
    groups, blocks = src_ref.shape[:2]
    wide = 2

    left_v[...] = jnp.concatenate(
        [src_ref[q, s].astype(jnp.float32) for s in range(blocks) for q in range(groups)], axis=0
    )

    def write(place):
        return pltpu.make_async_copy(out_v.at[place], out_ref.at[place], out_sem.at[place])

    for step in range(BIN // STEP_BINS):
        left = left_v[...]
        bin_of = lax.broadcasted_iota(jnp.int32, left.shape, 1) % BIN
        masked = jnp.concatenate(
            [
                jnp.where(bin_of == step * STEP_BINS + i, left, 0.0).astype(jnp.bfloat16)
                for i in range(STEP_BINS)
            ],
            axis=0,
        )
        for part in range(2):
            for z in range(0, planes, wide):
                right = jnp.concatenate([rhs_ref[part, z + u] for u in range(wide)], axis=1)
                both = jnp.dot(masked, right, preferred_element_type=jnp.float32)
                first = (part * planes + z) * LANES
                out_v[pl.ds(step * STEP_BINS, STEP_BINS), :, first : first + wide * LANES] = (
                    both.astype(jnp.bfloat16).reshape(STEP_BINS, left.shape[0], wide * LANES)
                )
        for i in range(STEP_BINS):
            write(step * STEP_BINS + i).start(priority=i % 2)

    def wait_body(place, carry):
        write(place).wait()
        return carry

    lax.fori_loop(0, BIN, wait_body, 0)


def per_device_kernels(records, quality, block_ids):
    devices = lax.axis_size("rcv")
    groups = devices // NB
    windows, channels, samples = records.shape
    sub_rows = channels // groups
    pack = LANES // sub_rows
    planes = devices // pack
    rows = 2 * BIN
    depth = windows * rows
    table = basis_table(samples, samples // 2).reshape(samples // 2, 2, NB * BIN)
    basis = jnp.asarray(np.ascontiguousarray(table.transpose(1, 0, 2)))
    padded_ids = jnp.pad(block_ids.reshape(1, -1), ((0, windows - 1), (0, LANES - channels - NSB)))
    small = jnp.concatenate([quality, padded_ids], axis=1)
    rhs, src = pl.pallas_call(
        exchange_kernel,
        out_shape=(
            jax.ShapeDtypeStruct((2, planes, depth, LANES), jnp.bfloat16),
            jax.ShapeDtypeStruct((groups, NSB, sub_rows, depth), jnp.bfloat16),
        ),
        in_specs=[
            pl.BlockSpec(memory_space=pltpu.VMEM),
            pl.BlockSpec(memory_space=pltpu.HBM),
            pl.BlockSpec(memory_space=pltpu.HBM),
        ],
        out_specs=(pl.BlockSpec(memory_space=pltpu.VMEM), pl.BlockSpec(memory_space=pltpu.VMEM)),
        scratch_shapes=[
            pltpu.VMEM(basis.shape, jnp.bfloat16),
            pltpu.VMEM((groups, 2, LANES, samples // 2), jnp.bfloat16),
            pltpu.VMEM((devices, rows, LANES), jnp.bfloat16),
            pltpu.VMEM((devices, rows, LANES), jnp.bfloat16),
            pltpu.VMEM((NSB, sub_rows, depth), jnp.bfloat16),
            pltpu.SemaphoreType.DMA((groups, 2 * windows)),
            pltpu.SemaphoreType.DMA((2,)),
            pltpu.SemaphoreType.DMA((devices,)),
            pltpu.SemaphoreType.DMA((devices,)),
            pltpu.SemaphoreType.DMA((2,)),
        ],
        compiler_params=pltpu.CompilerParams(
            collective_id=0, has_side_effects=True, vmem_limit_bytes=53 * 2**20
        ),
        name="spectra_exchange",
    )(small, basis, records)

    count = NSB * SBLK
    out_shape = (BIN, count, 2 * planes * LANES)
    joined = pl.pallas_call(
        product_kernel,
        out_shape=jax.ShapeDtypeStruct(out_shape, jnp.bfloat16),
        in_specs=[pl.BlockSpec(memory_space=pltpu.VMEM)] * 2,
        out_specs=pl.BlockSpec(memory_space=pltpu.HBM),
        scratch_shapes=[
            pltpu.VMEM((count, depth), jnp.float32),
            pltpu.VMEM(out_shape, jnp.bfloat16),
            pltpu.SemaphoreType.DMA((BIN,)),
        ],
        compiler_params=pltpu.CompilerParams(vmem_limit_bytes=40 * 2**20),
        name="cross_spectra",
    )(src, rhs)
    return joined[None]


def make_basis(samples):
    return jnp.asarray(basis_table(samples, samples))


def from_partner(value, axis, stride):
    mask = 2**stride
    pairs = [(source, source ^ mask) for source in range(lax.axis_size(axis))]
    return lax.ppermute(value, axis, pairs)


def per_device_general(records, quality, block_ids):
    devices = lax.axis_size("rcv")
    groups = devices // NB
    windows, channels, samples = records.shape
    sub_rows = channels // groups
    basis_table = make_basis(samples).reshape(samples, NB, 2 * BIN)
    rec_rows = records.reshape(windows, groups, sub_rows, samples)
    spectrum = jnp.einsum(
        "wqjs,sbm->bqwjm", rec_rows, basis_table, preferred_element_type=jnp.float32
    )
    band_power = jnp.sum(spectrum * spectrum, axis=-1) / BIN
    keep_gate = quality.reshape(windows, groups, sub_rows).transpose(1, 0, 2).astype(jnp.float32)
    scaling = keep_gate[None] * lax.rsqrt(band_power + 1e-05)
    whitened = (spectrum * scaling[..., None]).astype(jnp.bfloat16)
    send_buf = whitened.reshape(devices, windows, sub_rows * 2 * BIN)
    arrived = lax.all_to_all(send_buf, "rcv", split_axis=0, concat_axis=0, tiled=True)
    receivers = arrived.reshape(devices, windows, sub_rows, 2, BIN)
    my_index = lax.axis_index("rcv")
    per_block = channels // SBLK
    blk_rows = SBLK // sub_rows
    own_pieces = []
    for source_slot in range(NSB):
        owner_dev = block_ids[source_slot] // per_block
        own_pieces.append(lax.dynamic_index_in_dim(arrived, owner_dev, 0, keepdims=False))
    collected = jnp.stack(own_pieces)[None]
    my_group = my_index % groups
    for bit_level in range(groups.bit_length() - 1):
        partner = from_partner(collected, "rcv", bit_level)
        upper_side = my_group // 2**bit_level % 2 == 1
        low_half = jnp.where(upper_side, partner, collected)
        high_half = jnp.where(upper_side, collected, partner)
        collected = jnp.concatenate([low_half, high_half], axis=0)
    slices = []
    for source_slot in range(NSB):
        slices.append(collected[:, source_slot])
    src_band = jnp.stack(slices).reshape(NSB, blk_rows, windows, sub_rows, 2, BIN)
    source_count = NSB * SBLK
    group_width = devices * sub_rows
    left_side = src_band.transpose(5, 0, 1, 3, 2, 4).reshape(BIN, source_count, windows, 2)
    rec_cols = receivers.transpose(4, 1, 3, 0, 2).reshape(BIN, windows, 2, group_width)
    rotated = jnp.stack([rec_cols[:, :, 1], -rec_cols[:, :, 0]], axis=2)
    right_side = jnp.concatenate([rec_cols, rotated], axis=-1)
    joined = jnp.einsum("inwp,iwpk->ink", left_side, right_side, preferred_element_type=jnp.float32)
    return (joined * (1.0 / windows)).astype(jnp.bfloat16)[None]


def per_device(records, quality, block_ids):
    devices = lax.axis_size("rcv")
    windows, channels, samples = records.shape
    groups = devices // NB
    sub_rows = channels // groups
    pack = LANES // sub_rows
    fits = (
        groups == 2
        and channels == SBLK
        and windows == pack
        and sub_rows * pack == LANES
        and NSB * groups == pack
        and devices % (2 * pack) == 0
        and FLO % 2 == 0
        and samples % 2 == 0
    )
    return (per_device_kernels if fits else per_device_general)(records, quality, block_ids)


def solution(mesh):
    placed = (P("grp", "rcv", None), P("grp", "rcv"), P("grp"))
    return jax.shard_map(
        per_device,
        mesh=mesh,
        in_specs=placed,
        out_specs=P("rcv", "grp", None, None),
        check_vma=False,
    )
```

```python
import functools

import jax
import jax.numpy as jnp
import ml_dtypes
import numpy as np
from jax import lax
from jax.experimental import pallas as pl
from jax.experimental.pallas import tpu as pltpu
from jax.sharding import PartitionSpec as P

NB = 8
BIN = 32
FLO = 64
SBLK = 64
NSB = 2
LANES = 128


def basis_table(samples, count):
    times = np.arange(count, dtype=np.int64)
    bins = FLO + np.arange(NB * BIN, dtype=np.int64)
    phases = (times[:, None] * bins[None, :]) % samples
    angles = phases.astype(np.float64) * (2.0 * np.pi / samples)
    table = np.stack([np.cos(angles), -np.sin(angles)]).reshape(2, count, NB, BIN)
    table = table.transpose(1, 2, 0, 3).reshape(count, NB * 2 * BIN)
    return table.astype(np.float32).astype(ml_dtypes.bfloat16)


def lanes_to_rows(pieces, width):
    lane = lax.broadcasted_iota(jnp.int32, pieces[0].shape, 1) // width
    wide = [piece.astype(jnp.float32) for piece in pieces]
    result = []
    for w in range(len(pieces)):
        total = None
        for e, piece in enumerate(wide):
            shift = (e - w) * width % LANES
            moved = pltpu.roll(piece, shift, 1) if shift else piece
            total = moved if total is None else jnp.where(lane == e, moved, total)
        result.append(total)
    return result


def flipped(me, off):
    other, bit = me, 1
    while bit <= off:
        if off & bit:
            other = other + bit * (1 - 2 * (me // bit % 2))
        bit *= 2
    return other


def exchange_kernel(
    small_ref, basis_ref, records_ref, rhs_ref, src_ref,
    basis_v, rec_v, send_v, recv_v, own_v,
    load_sem, basis_sem, send_sem, recv_sem, src_sem,
):
    devices = recv_v.shape[0]
    windows, channels, samples = records_ref.shape
    groups = devices // NB
    sub_rows = channels // groups
    pack = LANES // sub_rows
    planes = devices // pack
    half = samples // 2
    rows = 2 * BIN
    me = lax.axis_index("rcv")

    barrier = pltpu.get_barrier_semaphore()
    for off in range(1, devices):
        pl.semaphore_signal(
            barrier, inc=1, device_id={"rcv": flipped(me, off)},
            device_id_type=pl.DeviceIdType.MESH,
        )

    loads = []
    for q in range(groups):
        for w in range(windows):
            place = q * windows + w
            for h in range(2):
                loads.append(
                    pltpu.make_async_copy(
                        records_ref.at[w, pl.ds(q * sub_rows, sub_rows), pl.ds(h * half, half)],
                        rec_v.at[h, pl.ds(place * sub_rows, sub_rows)],
                        load_sem.at[2 * place + h],
                    )
                )
    near_side = me // (devices // 2)
    sides = (1 - near_side, near_side)
    basis_loads = [
        pltpu.make_async_copy(basis_ref.at[side], basis_v.at[turn], basis_sem.at[turn])
        for turn, side in enumerate(sides)
    ]
    for turn, load in enumerate([basis_loads[0]] + loads + [basis_loads[1]]):
        load.start(priority=turn % 2)
    for load in loads:
        load.wait()

    keep = jnp.concatenate(
        [
            small_ref[w : w + 1, q * sub_rows : (q + 1) * sub_rows]
            for q in range(groups)
            for w in range(windows)
        ],
        axis=1,
    ).astype(jnp.float32)
    count = windows * channels

    def remote(peer):
        return pltpu.make_async_remote_copy(
            src_ref=send_v.at[peer], dst_ref=recv_v.at[me],
            send_sem=send_sem.at[peer], recv_sem=recv_sem.at[me],
            device_id={"rcv": peer}, device_id_type=pl.DeviceIdType.MESH,
        )

    def arrival(peer):
        return pltpu.make_async_remote_copy(
            src_ref=send_v.at[peer], dst_ref=recv_v.at[peer],
            send_sem=send_sem.at[peer], recv_sem=recv_sem.at[peer],
            device_id={"rcv": peer}, device_id_type=pl.DeviceIdType.MESH,
        )

    my_plane, my_place = me // pack, me % pack
    far_planes = [
        near_side * u + (1 - near_side) * (planes - 1 - u) for u in range(planes // 2)
    ]
    near_planes = [flipped(my_plane, u) for u in range(planes // 2 - 1, -1, -1)]
    for turn, side in enumerate(sides):
        basis_loads[turn].wait()
        halves = jnp.dot(
            rec_v[...].reshape(2 * count, half), basis_v[turn], preferred_element_type=jnp.float32
        )
        odd = lax.broadcasted_iota(jnp.int32, (count, halves.shape[1]), 1) % 2 == 1
        late = halves[count:]
        spectra = (halves[:count] + jnp.where(odd, -late, late)).T
        for b in range(NB // 2):
            spectrum = spectra[b * rows : (b + 1) * rows]
            power = jnp.sum(spectrum * spectrum, axis=0, keepdims=True) / BIN
            white = (spectrum * (keep * lax.rsqrt(power + 1e-05))).astype(jnp.bfloat16)
            for q in range(groups):
                send_v[side * (devices // 2) + b * groups + q] = white[:, q * LANES : (q + 1) * LANES]
        if turn == 0:
            pl.semaphore_wait(barrier, devices - 1)
        if turn == 0:
            for e in range(pack - 1, -1, -1):
                for plane in far_planes[: planes // 4]:
                    remote(plane * pack + flipped(my_place, e)).start()
    for e in range(pack - 1, -1, -1):
        for far, near in zip(far_planes[planes // 4 :], near_planes):
            remote(far * pack + flipped(my_place, e)).start()
            remote(near * pack + flipped(my_place, e)).start()
    for near in near_planes[planes // 4 :]:
        own = near is near_planes[-1]
        for e in range(pack - 1, 0 if own else -1, -1):
            remote(near * pack + flipped(my_place, e)).start()
    recv_v[me] = send_v[me]

    ordered = near_planes[::-1] + far_planes
    for turn, plane in enumerate(ordered):
        for e in range(0 if turn else 1, pack):
            arrival(plane * pack + flipped(my_place, e)).wait_recv()
        if turn == planes - 1:
            for s in range(NSB):
                turned = recv_v[small_ref[0, channels + s]].astype(jnp.float32).T * (1.0 / windows)
                own_v[s] = jnp.concatenate(
                    [turned[w * sub_rows : (w + 1) * sub_rows] for w in range(windows)], axis=1
                ).astype(jnp.bfloat16)
            swap = pltpu.make_async_remote_copy(
                src_ref=own_v, dst_ref=src_ref.at[me % groups],
                send_sem=src_sem.at[0], recv_sem=src_sem.at[1],
                device_id={"rcv": flipped(me, 1)}, device_id_type=pl.DeviceIdType.MESH,
            )
            swap.start()
            src_ref[me % groups] = own_v[...]
        by_window = lanes_to_rows([recv_v[plane * pack + e] for e in range(pack)], sub_rows)
        for w, block in enumerate(by_window):
            real, imag = block[:BIN], block[BIN:]
            rhs_ref[0, plane, w * rows : w * rows + BIN] = real.astype(jnp.bfloat16)
            rhs_ref[0, plane, w * rows + BIN : (w + 1) * rows] = imag.astype(jnp.bfloat16)
            rhs_ref[1, plane, w * rows : w * rows + BIN] = imag.astype(jnp.bfloat16)
            rhs_ref[1, plane, w * rows + BIN : (w + 1) * rows] = (-real).astype(jnp.bfloat16)
    for off in range(1, devices):
        remote(flipped(me, off)).wait_send()
    swap.wait()


STEP_BINS = 4


def product_kernel(src_ref, rhs_ref, out_ref, left_v, out_v, out_sem):
    planes = rhs_ref.shape[1]
    groups, blocks = src_ref.shape[:2]
    wide = 2

    left_v[...] = jnp.concatenate(
        [src_ref[q, s].astype(jnp.float32) for s in range(blocks) for q in range(groups)], axis=0
    )

    def write(place):
        return pltpu.make_async_copy(out_v.at[place], out_ref.at[place], out_sem.at[place])

    for step in range(BIN // STEP_BINS):
        left = left_v[...]
        bin_of = lax.broadcasted_iota(jnp.int32, left.shape, 1) % BIN
        masked = jnp.concatenate(
            [
                jnp.where(bin_of == step * STEP_BINS + i, left, 0.0).astype(jnp.bfloat16)
                for i in range(STEP_BINS)
            ],
            axis=0,
        )
        for part in range(2):
            for z in range(0, planes, wide):
                right = jnp.concatenate([rhs_ref[part, z + u] for u in range(wide)], axis=1)
                both = jnp.dot(masked, right, preferred_element_type=jnp.float32)
                first = (part * planes + z) * LANES
                out_v[pl.ds(step * STEP_BINS, STEP_BINS), :, first : first + wide * LANES] = (
                    both.astype(jnp.bfloat16).reshape(STEP_BINS, left.shape[0], wide * LANES)
                )
        for i in range(STEP_BINS):
            write(step * STEP_BINS + i).start(priority=i % 2)

    def wait_body(place, carry):
        write(place).wait()
        return carry

    lax.fori_loop(0, BIN, wait_body, 0)


def per_device_kernels(records, quality, block_ids):
    devices = lax.axis_size("rcv")
    groups = devices // NB
    windows, channels, samples = records.shape
    sub_rows = channels // groups
    pack = LANES // sub_rows
    planes = devices // pack
    rows = 2 * BIN
    depth = windows * rows
    table = basis_table(samples, samples // 2).reshape(samples // 2, 2, NB * BIN)
    basis = jnp.asarray(np.ascontiguousarray(table.transpose(1, 0, 2)))
    padded_ids = jnp.pad(block_ids.reshape(1, -1), ((0, windows - 1), (0, LANES - channels - NSB)))
    small = jnp.concatenate([quality, padded_ids], axis=1)
    rhs, src = pl.pallas_call(
        exchange_kernel,
        out_shape=(
            jax.ShapeDtypeStruct((2, planes, depth, LANES), jnp.bfloat16),
            jax.ShapeDtypeStruct((groups, NSB, sub_rows, depth), jnp.bfloat16),
        ),
        in_specs=[
            pl.BlockSpec(memory_space=pltpu.VMEM),
            pl.BlockSpec(memory_space=pltpu.HBM),
            pl.BlockSpec(memory_space=pltpu.HBM),
        ],
        out_specs=(pl.BlockSpec(memory_space=pltpu.VMEM), pl.BlockSpec(memory_space=pltpu.VMEM)),
        scratch_shapes=[
            pltpu.VMEM(basis.shape, jnp.bfloat16),
            pltpu.VMEM((2, windows * channels, samples // 2), jnp.bfloat16),
            pltpu.VMEM((devices, rows, LANES), jnp.bfloat16),
            pltpu.VMEM((devices, rows, LANES), jnp.bfloat16),
            pltpu.VMEM((NSB, sub_rows, depth), jnp.bfloat16),
            pltpu.SemaphoreType.DMA((2 * groups * windows,)),
            pltpu.SemaphoreType.DMA((2,)),
            pltpu.SemaphoreType.DMA((devices,)),
            pltpu.SemaphoreType.DMA((devices,)),
            pltpu.SemaphoreType.DMA((2,)),
        ],
        compiler_params=pltpu.CompilerParams(
            collective_id=0, has_side_effects=True, vmem_limit_bytes=53 * 2**20
        ),
        name="spectra_exchange",
    )(small, basis, records)

    count = NSB * SBLK
    out_shape = (BIN, count, 2 * planes * LANES)
    joined = pl.pallas_call(
        product_kernel,
        out_shape=jax.ShapeDtypeStruct(out_shape, jnp.bfloat16),
        in_specs=[pl.BlockSpec(memory_space=pltpu.VMEM)] * 2,
        out_specs=pl.BlockSpec(memory_space=pltpu.HBM),
        scratch_shapes=[
            pltpu.VMEM((count, depth), jnp.float32),
            pltpu.VMEM(out_shape, jnp.bfloat16),
            pltpu.SemaphoreType.DMA((BIN,)),
        ],
        compiler_params=pltpu.CompilerParams(vmem_limit_bytes=40 * 2**20),
        name="cross_spectra",
    )(src, rhs)
    return joined[None]


def make_basis(samples):
    return jnp.asarray(basis_table(samples, samples))


def from_partner(value, axis, stride):
    mask = 2**stride
    pairs = [(source, source ^ mask) for source in range(lax.axis_size(axis))]
    return lax.ppermute(value, axis, pairs)


def per_device_general(records, quality, block_ids):
    devices = lax.axis_size("rcv")
    groups = devices // NB
    windows, channels, samples = records.shape
    sub_rows = channels // groups
    basis_table = make_basis(samples).reshape(samples, NB, 2 * BIN)
    rec_rows = records.reshape(windows, groups, sub_rows, samples)
    spectrum = jnp.einsum(
        "wqjs,sbm->bqwjm", rec_rows, basis_table, preferred_element_type=jnp.float32
    )
    band_power = jnp.sum(spectrum * spectrum, axis=-1) / BIN
    keep_gate = quality.reshape(windows, groups, sub_rows).transpose(1, 0, 2).astype(jnp.float32)
    scaling = keep_gate[None] * lax.rsqrt(band_power + 1e-05)
    whitened = (spectrum * scaling[..., None]).astype(jnp.bfloat16)
    send_buf = whitened.reshape(devices, windows, sub_rows * 2 * BIN)
    arrived = lax.all_to_all(send_buf, "rcv", split_axis=0, concat_axis=0, tiled=True)
    receivers = arrived.reshape(devices, windows, sub_rows, 2, BIN)
    my_index = lax.axis_index("rcv")
    per_block = channels // SBLK
    blk_rows = SBLK // sub_rows
    own_pieces = []
    for source_slot in range(NSB):
        owner_dev = block_ids[source_slot] // per_block
        own_pieces.append(lax.dynamic_index_in_dim(arrived, owner_dev, 0, keepdims=False))
    collected = jnp.stack(own_pieces)[None]
    my_group = my_index % groups
    for bit_level in range(groups.bit_length() - 1):
        partner = from_partner(collected, "rcv", bit_level)
        upper_side = my_group // 2**bit_level % 2 == 1
        low_half = jnp.where(upper_side, partner, collected)
        high_half = jnp.where(upper_side, collected, partner)
        collected = jnp.concatenate([low_half, high_half], axis=0)
    slices = []
    for source_slot in range(NSB):
        slices.append(collected[:, source_slot])
    src_band = jnp.stack(slices).reshape(NSB, blk_rows, windows, sub_rows, 2, BIN)
    source_count = NSB * SBLK
    group_width = devices * sub_rows
    left_side = src_band.transpose(5, 0, 1, 3, 2, 4).reshape(BIN, source_count, windows, 2)
    rec_cols = receivers.transpose(4, 1, 3, 0, 2).reshape(BIN, windows, 2, group_width)
    rotated = jnp.stack([rec_cols[:, :, 1], -rec_cols[:, :, 0]], axis=2)
    right_side = jnp.concatenate([rec_cols, rotated], axis=-1)
    joined = jnp.einsum("inwp,iwpk->ink", left_side, right_side, preferred_element_type=jnp.float32)
    return (joined * (1.0 / windows)).astype(jnp.bfloat16)[None]


def per_device(records, quality, block_ids):
    devices = lax.axis_size("rcv")
    windows, channels, samples = records.shape
    groups = devices // NB
    sub_rows = channels // groups
    pack = LANES // sub_rows
    fits = (
        groups == 2
        and channels == SBLK
        and windows == pack
        and sub_rows * pack == LANES
        and NSB * groups == pack
        and devices % (2 * pack) == 0
        and FLO % 2 == 0
        and samples % 2 == 0
    )
    return (per_device_kernels if fits else per_device_general)(records, quality, block_ids)


def solution(mesh):
    placed = (P("grp", "rcv", None), P("grp", "rcv"), P("grp"))
    return jax.shard_map(
        per_device,
        mesh=mesh,
        in_specs=placed,
        out_specs=P("rcv", "grp", None, None),
        check_vma=False,
    )
```

```python
import functools

import jax
import jax.numpy as jnp
import ml_dtypes
import numpy as np
from jax import lax
from jax.experimental import pallas as pl
from jax.experimental.pallas import tpu as pltpu
from jax.sharding import PartitionSpec as P

NB = 8
BIN = 32
FLO = 64
SBLK = 64
NSB = 2
LANES = 128


def basis_table(samples, count):
    times = np.arange(count, dtype=np.int64)
    bins = FLO + np.arange(NB * BIN, dtype=np.int64)
    phases = (times[:, None] * bins[None, :]) % samples
    angles = phases.astype(np.float64) * (2.0 * np.pi / samples)
    table = np.stack([np.cos(angles), -np.sin(angles)]).reshape(2, count, NB, BIN)
    table = table.transpose(1, 2, 0, 3).reshape(count, NB * 2 * BIN)
    return table.astype(np.float32).astype(ml_dtypes.bfloat16)


def lanes_to_rows(pieces, width):
    lane = lax.broadcasted_iota(jnp.int32, pieces[0].shape, 1) // width
    wide = [piece.astype(jnp.float32) for piece in pieces]
    result = []
    for w in range(len(pieces)):
        total = None
        for e, piece in enumerate(wide):
            shift = (e - w) * width % LANES
            moved = pltpu.roll(piece, shift, 1) if shift else piece
            total = moved if total is None else jnp.where(lane == e, moved, total)
        result.append(total)
    return result


def flipped(me, off):
    other, bit = me, 1
    while bit <= off:
        if off & bit:
            other = other + bit * (1 - 2 * (me // bit % 2))
        bit *= 2
    return other


def exchange_kernel(
    small_ref, basis_ref, records_ref, rhs_ref, src_ref,
    basis_v, rec_v, send_v, recv_v, own_v,
    load_sem, basis_sem, send_sem, recv_sem, src_sem,
):
    devices = recv_v.shape[0]
    windows, channels, samples = records_ref.shape
    groups = devices // NB
    sub_rows = channels // groups
    pack = LANES // sub_rows
    planes = devices // pack
    half = samples // 2
    rows = 2 * BIN
    me = lax.axis_index("rcv")

    barrier = pltpu.get_barrier_semaphore()
    for off in range(1, devices):
        pl.semaphore_signal(
            barrier, inc=1, device_id={"rcv": flipped(me, off)},
            device_id_type=pl.DeviceIdType.MESH,
        )

    loads = []
    for q in range(groups):
        for w in range(windows):
            place = q * windows + w
            for h in range(2):
                loads.append(
                    pltpu.make_async_copy(
                        records_ref.at[w, pl.ds(q * sub_rows, sub_rows), pl.ds(h * half, half)],
                        rec_v.at[h, pl.ds(place * sub_rows, sub_rows)],
                        load_sem.at[2 * place + h],
                    )
                )
    near_side = me // (devices // 2)
    sides = (1 - near_side, near_side)
    basis_loads = [
        pltpu.make_async_copy(basis_ref.at[side], basis_v.at[turn], basis_sem.at[turn])
        for turn, side in enumerate(sides)
    ]
    for turn, load in enumerate([basis_loads[0]] + loads + [basis_loads[1]]):
        load.start(priority=turn % 2)
    for load in loads:
        load.wait()

    keep = jnp.concatenate(
        [
            small_ref[w : w + 1, q * sub_rows : (q + 1) * sub_rows]
            for q in range(groups)
            for w in range(windows)
        ],
        axis=1,
    ).astype(jnp.float32)
    count = windows * channels

    def remote(peer):
        return pltpu.make_async_remote_copy(
            src_ref=send_v.at[peer], dst_ref=recv_v.at[me],
            send_sem=send_sem.at[peer], recv_sem=recv_sem.at[me],
            device_id={"rcv": peer}, device_id_type=pl.DeviceIdType.MESH,
        )

    def arrival(peer):
        return pltpu.make_async_remote_copy(
            src_ref=send_v.at[peer], dst_ref=recv_v.at[peer],
            send_sem=send_sem.at[peer], recv_sem=recv_sem.at[peer],
            device_id={"rcv": peer}, device_id_type=pl.DeviceIdType.MESH,
        )

    my_plane, my_place = me // pack, me % pack
    far_planes = [
        near_side * u + (1 - near_side) * (planes - 1 - u) for u in range(planes // 2)
    ]
    outer_near = [
        near_side * (planes - 1 - u) + (1 - near_side) * u for u in range(planes // 2)
    ]

    def send_plane(plane):
        for e in range(pack - 1, 0, -1):
            remote(plane * pack + flipped(my_place, e)).start()
        pl.when(plane != my_plane)(remote(plane * pack + my_place).start)

    near_planes = [flipped(my_plane, u) for u in range(planes // 2 - 1, -1, -1)]
    for turn, side in enumerate(sides):
        basis_loads[turn].wait()
        halves = jnp.dot(
            rec_v[...].reshape(2 * count, half), basis_v[turn], preferred_element_type=jnp.float32
        )
        odd = lax.broadcasted_iota(jnp.int32, (count, halves.shape[1]), 1) % 2 == 1
        late = halves[count:]
        spectra = (halves[:count] + jnp.where(odd, -late, late)).T
        for b in range(NB // 2):
            spectrum = spectra[b * rows : (b + 1) * rows]
            power = jnp.sum(spectrum * spectrum, axis=0, keepdims=True) / BIN
            white = (spectrum * (keep * lax.rsqrt(power + 1e-05))).astype(jnp.bfloat16)
            for q in range(groups):
                send_v[side * (devices // 2) + b * groups + q] = white[:, q * LANES : (q + 1) * LANES]
        if turn == 0:
            pl.semaphore_wait(barrier, devices - 1)
        if turn == 0:
            send_plane(far_planes[0])
    for u in range(planes // 2):
        if u:
            send_plane(far_planes[u])
        send_plane(outer_near[u])
    recv_v[me] = send_v[me]

    ordered = near_planes[::-1] + far_planes
    for turn, plane in enumerate(ordered):
        for e in range(0 if turn else 1, pack):
            arrival(plane * pack + flipped(my_place, e)).wait_recv()
        if turn == planes - 1:
            for s in range(NSB):
                turned = recv_v[small_ref[0, channels + s]].astype(jnp.float32).T * (1.0 / windows)
                own_v[s] = jnp.concatenate(
                    [turned[w * sub_rows : (w + 1) * sub_rows] for w in range(windows)], axis=1
                ).astype(jnp.bfloat16)
            swap = pltpu.make_async_remote_copy(
                src_ref=own_v, dst_ref=src_ref.at[me % groups],
                send_sem=src_sem.at[0], recv_sem=src_sem.at[1],
                device_id={"rcv": flipped(me, 1)}, device_id_type=pl.DeviceIdType.MESH,
            )
            swap.start()
            src_ref[me % groups] = own_v[...]
        by_window = lanes_to_rows([recv_v[plane * pack + e] for e in range(pack)], sub_rows)
        for w, block in enumerate(by_window):
            real, imag = block[:BIN], block[BIN:]
            rhs_ref[0, plane, w * rows : w * rows + BIN] = real.astype(jnp.bfloat16)
            rhs_ref[0, plane, w * rows + BIN : (w + 1) * rows] = imag.astype(jnp.bfloat16)
            rhs_ref[1, plane, w * rows : w * rows + BIN] = imag.astype(jnp.bfloat16)
            rhs_ref[1, plane, w * rows + BIN : (w + 1) * rows] = (-real).astype(jnp.bfloat16)
    for off in range(1, devices):
        remote(flipped(me, off)).wait_send()
    swap.wait()


STEP_BINS = 4


def product_kernel(src_ref, rhs_ref, out_ref, left_v, out_v, out_sem):
    planes = rhs_ref.shape[1]
    groups, blocks = src_ref.shape[:2]
    wide = 2

    left_v[...] = jnp.concatenate(
        [src_ref[q, s].astype(jnp.float32) for s in range(blocks) for q in range(groups)], axis=0
    )

    def write(place):
        return pltpu.make_async_copy(out_v.at[place], out_ref.at[place], out_sem.at[place])

    for step in range(BIN // STEP_BINS):
        left = left_v[...]
        bin_of = lax.broadcasted_iota(jnp.int32, left.shape, 1) % BIN
        masked = jnp.concatenate(
            [
                jnp.where(bin_of == step * STEP_BINS + i, left, 0.0).astype(jnp.bfloat16)
                for i in range(STEP_BINS)
            ],
            axis=0,
        )
        for part in range(2):
            for z in range(0, planes, wide):
                right = jnp.concatenate([rhs_ref[part, z + u] for u in range(wide)], axis=1)
                both = jnp.dot(masked, right, preferred_element_type=jnp.float32)
                first = (part * planes + z) * LANES
                out_v[pl.ds(step * STEP_BINS, STEP_BINS), :, first : first + wide * LANES] = (
                    both.astype(jnp.bfloat16).reshape(STEP_BINS, left.shape[0], wide * LANES)
                )
        for i in range(STEP_BINS):
            write(step * STEP_BINS + i).start(priority=i % 2)

    def wait_body(place, carry):
        write(place).wait()
        return carry

    lax.fori_loop(0, BIN, wait_body, 0)


def per_device_kernels(records, quality, block_ids):
    devices = lax.axis_size("rcv")
    groups = devices // NB
    windows, channels, samples = records.shape
    sub_rows = channels // groups
    pack = LANES // sub_rows
    planes = devices // pack
    rows = 2 * BIN
    depth = windows * rows
    table = basis_table(samples, samples // 2).reshape(samples // 2, 2, NB * BIN)
    basis = jnp.asarray(np.ascontiguousarray(table.transpose(1, 0, 2)))
    padded_ids = jnp.pad(block_ids.reshape(1, -1), ((0, windows - 1), (0, LANES - channels - NSB)))
    small = jnp.concatenate([quality, padded_ids], axis=1)
    rhs, src = pl.pallas_call(
        exchange_kernel,
        out_shape=(
            jax.ShapeDtypeStruct((2, planes, depth, LANES), jnp.bfloat16),
            jax.ShapeDtypeStruct((groups, NSB, sub_rows, depth), jnp.bfloat16),
        ),
        in_specs=[
            pl.BlockSpec(memory_space=pltpu.VMEM),
            pl.BlockSpec(memory_space=pltpu.HBM),
            pl.BlockSpec(memory_space=pltpu.HBM),
        ],
        out_specs=(pl.BlockSpec(memory_space=pltpu.VMEM), pl.BlockSpec(memory_space=pltpu.VMEM)),
        scratch_shapes=[
            pltpu.VMEM(basis.shape, jnp.bfloat16),
            pltpu.VMEM((2, windows * channels, samples // 2), jnp.bfloat16),
            pltpu.VMEM((devices, rows, LANES), jnp.bfloat16),
            pltpu.VMEM((devices, rows, LANES), jnp.bfloat16),
            pltpu.VMEM((NSB, sub_rows, depth), jnp.bfloat16),
            pltpu.SemaphoreType.DMA((2 * groups * windows,)),
            pltpu.SemaphoreType.DMA((2,)),
            pltpu.SemaphoreType.DMA((devices,)),
            pltpu.SemaphoreType.DMA((devices,)),
            pltpu.SemaphoreType.DMA((2,)),
        ],
        compiler_params=pltpu.CompilerParams(
            collective_id=0, has_side_effects=True, vmem_limit_bytes=53 * 2**20
        ),
        name="spectra_exchange",
    )(small, basis, records)

    count = NSB * SBLK
    out_shape = (BIN, count, 2 * planes * LANES)
    joined = pl.pallas_call(
        product_kernel,
        out_shape=jax.ShapeDtypeStruct(out_shape, jnp.bfloat16),
        in_specs=[pl.BlockSpec(memory_space=pltpu.VMEM)] * 2,
        out_specs=pl.BlockSpec(memory_space=pltpu.HBM),
        scratch_shapes=[
            pltpu.VMEM((count, depth), jnp.float32),
            pltpu.VMEM(out_shape, jnp.bfloat16),
            pltpu.SemaphoreType.DMA((BIN,)),
        ],
        compiler_params=pltpu.CompilerParams(vmem_limit_bytes=40 * 2**20),
        name="cross_spectra",
    )(src, rhs)
    return joined[None]


def make_basis(samples):
    return jnp.asarray(basis_table(samples, samples))


def from_partner(value, axis, stride):
    mask = 2**stride
    pairs = [(source, source ^ mask) for source in range(lax.axis_size(axis))]
    return lax.ppermute(value, axis, pairs)


def per_device_general(records, quality, block_ids):
    devices = lax.axis_size("rcv")
    groups = devices // NB
    windows, channels, samples = records.shape
    sub_rows = channels // groups
    basis_table = make_basis(samples).reshape(samples, NB, 2 * BIN)
    rec_rows = records.reshape(windows, groups, sub_rows, samples)
    spectrum = jnp.einsum(
        "wqjs,sbm->bqwjm", rec_rows, basis_table, preferred_element_type=jnp.float32
    )
    band_power = jnp.sum(spectrum * spectrum, axis=-1) / BIN
    keep_gate = quality.reshape(windows, groups, sub_rows).transpose(1, 0, 2).astype(jnp.float32)
    scaling = keep_gate[None] * lax.rsqrt(band_power + 1e-05)
    whitened = (spectrum * scaling[..., None]).astype(jnp.bfloat16)
    send_buf = whitened.reshape(devices, windows, sub_rows * 2 * BIN)
    arrived = lax.all_to_all(send_buf, "rcv", split_axis=0, concat_axis=0, tiled=True)
    receivers = arrived.reshape(devices, windows, sub_rows, 2, BIN)
    my_index = lax.axis_index("rcv")
    per_block = channels // SBLK
    blk_rows = SBLK // sub_rows
    own_pieces = []
    for source_slot in range(NSB):
        owner_dev = block_ids[source_slot] // per_block
        own_pieces.append(lax.dynamic_index_in_dim(arrived, owner_dev, 0, keepdims=False))
    collected = jnp.stack(own_pieces)[None]
    my_group = my_index % groups
    for bit_level in range(groups.bit_length() - 1):
        partner = from_partner(collected, "rcv", bit_level)
        upper_side = my_group // 2**bit_level % 2 == 1
        low_half = jnp.where(upper_side, partner, collected)
        high_half = jnp.where(upper_side, collected, partner)
        collected = jnp.concatenate([low_half, high_half], axis=0)
    slices = []
    for source_slot in range(NSB):
        slices.append(collected[:, source_slot])
    src_band = jnp.stack(slices).reshape(NSB, blk_rows, windows, sub_rows, 2, BIN)
    source_count = NSB * SBLK
    group_width = devices * sub_rows
    left_side = src_band.transpose(5, 0, 1, 3, 2, 4).reshape(BIN, source_count, windows, 2)
    rec_cols = receivers.transpose(4, 1, 3, 0, 2).reshape(BIN, windows, 2, group_width)
    rotated = jnp.stack([rec_cols[:, :, 1], -rec_cols[:, :, 0]], axis=2)
    right_side = jnp.concatenate([rec_cols, rotated], axis=-1)
    joined = jnp.einsum("inwp,iwpk->ink", left_side, right_side, preferred_element_type=jnp.float32)
    return (joined * (1.0 / windows)).astype(jnp.bfloat16)[None]


def per_device(records, quality, block_ids):
    devices = lax.axis_size("rcv")
    windows, channels, samples = records.shape
    groups = devices // NB
    sub_rows = channels // groups
    pack = LANES // sub_rows
    fits = (
        groups == 2
        and channels == SBLK
        and windows == pack
        and sub_rows * pack == LANES
        and NSB * groups == pack
        and devices % (2 * pack) == 0
        and FLO % 2 == 0
        and samples % 2 == 0
    )
    return (per_device_kernels if fits else per_device_general)(records, quality, block_ids)


def solution(mesh):
    placed = (P("grp", "rcv", None), P("grp", "rcv"), P("grp"))
    return jax.shard_map(
        per_device,
        mesh=mesh,
        in_specs=placed,
        out_specs=P("rcv", "grp", None, None),
        check_vma=False,
    )
```

```python
import functools

import jax
import jax.numpy as jnp
import ml_dtypes
import numpy as np
from jax import lax
from jax.experimental import pallas as pl
from jax.experimental.pallas import tpu as pltpu
from jax.sharding import PartitionSpec as P

NB = 8
BIN = 32
FLO = 64
SBLK = 64
NSB = 2
LANES = 128


def basis_table(samples, count):
    times = np.arange(count, dtype=np.int64)
    bins = FLO + np.arange(NB * BIN, dtype=np.int64)
    phases = (times[:, None] * bins[None, :]) % samples
    angles = phases.astype(np.float64) * (2.0 * np.pi / samples)
    table = np.stack([np.cos(angles), -np.sin(angles)]).reshape(2, count, NB, BIN)
    table = table.transpose(1, 2, 0, 3).reshape(count, NB * 2 * BIN)
    return table.astype(np.float32).astype(ml_dtypes.bfloat16)


def lanes_to_rows(pieces, width):
    lane = lax.broadcasted_iota(jnp.int32, pieces[0].shape, 1) // width
    wide = [piece.astype(jnp.float32) for piece in pieces]
    result = []
    for w in range(len(pieces)):
        total = None
        for e, piece in enumerate(wide):
            shift = (e - w) * width % LANES
            moved = pltpu.roll(piece, shift, 1) if shift else piece
            total = moved if total is None else jnp.where(lane == e, moved, total)
        result.append(total)
    return result


def flipped(me, off):
    other, bit = me, 1
    while bit <= off:
        if off & bit:
            other = other + bit * (1 - 2 * (me // bit % 2))
        bit *= 2
    return other


def exchange_kernel(
    small_ref, basis_ref, records_ref, rhs_ref, src_ref,
    basis_v, rec_v, send_v, recv_v, own_v,
    load_sem, basis_sem, send_sem, recv_sem, src_sem,
):
    devices = recv_v.shape[0]
    windows, channels, samples = records_ref.shape
    groups = devices // NB
    sub_rows = channels // groups
    pack = LANES // sub_rows
    planes = devices // pack
    half = samples // 2
    rows = 2 * BIN
    me = lax.axis_index("rcv")

    barrier = pltpu.get_barrier_semaphore()
    for off in range(1, devices):
        pl.semaphore_signal(
            barrier, inc=1, device_id={"rcv": flipped(me, off)},
            device_id_type=pl.DeviceIdType.MESH,
        )

    loads = []
    for q in range(groups):
        for w in range(windows):
            place = q * windows + w
            for h in range(2):
                loads.append(
                    pltpu.make_async_copy(
                        records_ref.at[w, pl.ds(q * sub_rows, sub_rows), pl.ds(h * half, half)],
                        rec_v.at[h, pl.ds(place * sub_rows, sub_rows)],
                        load_sem.at[2 * place + h],
                    )
                )
    near_side = me // (devices // 2)
    sides = (1 - near_side, near_side)
    basis_loads = [
        pltpu.make_async_copy(basis_ref.at[side], basis_v.at[turn], basis_sem.at[turn])
        for turn, side in enumerate(sides)
    ]
    for turn, load in enumerate([basis_loads[0]] + loads + [basis_loads[1]]):
        load.start(priority=turn % 2)
    for load in loads:
        load.wait()

    keep = jnp.concatenate(
        [
            small_ref[w : w + 1, q * sub_rows : (q + 1) * sub_rows]
            for q in range(groups)
            for w in range(windows)
        ],
        axis=1,
    ).astype(jnp.float32)
    count = windows * channels

    def remote(peer):
        return pltpu.make_async_remote_copy(
            src_ref=send_v.at[peer], dst_ref=recv_v.at[me],
            send_sem=send_sem.at[peer], recv_sem=recv_sem.at[me],
            device_id={"rcv": peer}, device_id_type=pl.DeviceIdType.MESH,
        )

    def arrival(peer):
        return pltpu.make_async_remote_copy(
            src_ref=send_v.at[peer], dst_ref=recv_v.at[peer],
            send_sem=send_sem.at[peer], recv_sem=recv_sem.at[peer],
            device_id={"rcv": peer}, device_id_type=pl.DeviceIdType.MESH,
        )

    my_plane, my_place = me // pack, me % pack
    far_planes = [
        near_side * u + (1 - near_side) * (planes - 1 - u) for u in range(planes // 2)
    ]
    outer_near = [
        near_side * (planes - 1 - u) + (1 - near_side) * u for u in range(planes // 2)
    ]

    def send_plane(plane):
        for e in range(pack - 1, 0, -1):
            remote(plane * pack + flipped(my_place, e)).start()
        pl.when(plane != my_plane)(remote(plane * pack + my_place).start)

    near_planes = [flipped(my_plane, u) for u in range(planes // 2 - 1, -1, -1)]
    for turn, side in enumerate(sides):
        basis_loads[turn].wait()
        halves = jnp.dot(
            rec_v[...].reshape(2 * count, half), basis_v[turn], preferred_element_type=jnp.float32
        )
        odd = lax.broadcasted_iota(jnp.int32, (count, halves.shape[1]), 1) % 2 == 1
        late = halves[count:]
        spectra = (halves[:count] + jnp.where(odd, -late, late)).T
        for b in range(NB // 2):
            spectrum = spectra[b * rows : (b + 1) * rows]
            power = jnp.sum(spectrum * spectrum, axis=0, keepdims=True) / BIN
            white = (spectrum * (keep * lax.rsqrt(power + 1e-05))).astype(jnp.bfloat16)
            for q in range(groups):
                send_v[side * (devices // 2) + b * groups + q] = white[:, q * LANES : (q + 1) * LANES]
        if turn == 0:
            pl.semaphore_wait(barrier, devices - 1)
        if turn == 0:
            send_plane(far_planes[0])
    for u in range(planes // 2):
        if u:
            for e in range(pack):
                remote(far_planes[u - 1] * pack + e).wait_send()
            send_plane(far_planes[u])
        send_plane(outer_near[u])
    recv_v[me] = send_v[me]

    ordered = near_planes[::-1] + far_planes
    for turn, plane in enumerate(ordered):
        for e in range(0 if turn else 1, pack):
            arrival(plane * pack + flipped(my_place, e)).wait_recv()
        if turn == planes - 1:
            for s in range(NSB):
                turned = recv_v[small_ref[0, channels + s]].astype(jnp.float32).T * (1.0 / windows)
                own_v[s] = jnp.concatenate(
                    [turned[w * sub_rows : (w + 1) * sub_rows] for w in range(windows)], axis=1
                ).astype(jnp.bfloat16)
            swap = pltpu.make_async_remote_copy(
                src_ref=own_v, dst_ref=src_ref.at[me % groups],
                send_sem=src_sem.at[0], recv_sem=src_sem.at[1],
                device_id={"rcv": flipped(me, 1)}, device_id_type=pl.DeviceIdType.MESH,
            )
            swap.start()
            src_ref[me % groups] = own_v[...]
        by_window = lanes_to_rows([recv_v[plane * pack + e] for e in range(pack)], sub_rows)
        for w, block in enumerate(by_window):
            real, imag = block[:BIN], block[BIN:]
            rhs_ref[0, plane, w * rows : w * rows + BIN] = real.astype(jnp.bfloat16)
            rhs_ref[0, plane, w * rows + BIN : (w + 1) * rows] = imag.astype(jnp.bfloat16)
            rhs_ref[1, plane, w * rows : w * rows + BIN] = imag.astype(jnp.bfloat16)
            rhs_ref[1, plane, w * rows + BIN : (w + 1) * rows] = (-real).astype(jnp.bfloat16)
    for off in range(1, devices // 2):
        remote(flipped(me, off)).wait_send()
    for e in range(pack):
        remote(far_planes[-1] * pack + e).wait_send()
    swap.wait()


STEP_BINS = 2


def product_kernel(src_ref, rhs_ref, out_ref, left_v, out_v, out_sem):
    planes = rhs_ref.shape[1]
    groups, blocks = src_ref.shape[:2]
    wide = 2

    left_v[...] = jnp.concatenate(
        [src_ref[q, s].astype(jnp.float32) for s in range(blocks) for q in range(groups)], axis=0
    )

    def write(place):
        return pltpu.make_async_copy(out_v.at[place], out_ref.at[place], out_sem.at[place])

    for step in range(BIN // STEP_BINS):
        left = left_v[...]
        bin_of = lax.broadcasted_iota(jnp.int32, left.shape, 1) % BIN
        masked = jnp.concatenate(
            [
                jnp.where(bin_of == step * STEP_BINS + i, left, 0.0).astype(jnp.bfloat16)
                for i in range(STEP_BINS)
            ],
            axis=0,
        )
        for part in range(2):
            for z in range(0, planes, wide):
                right = jnp.concatenate([rhs_ref[part, z + u] for u in range(wide)], axis=1)
                both = jnp.dot(masked, right, preferred_element_type=jnp.float32)
                first = (part * planes + z) * LANES
                out_v[pl.ds(step * STEP_BINS, STEP_BINS), :, first : first + wide * LANES] = (
                    both.astype(jnp.bfloat16).reshape(STEP_BINS, left.shape[0], wide * LANES)
                )
        for i in range(STEP_BINS):
            write(step * STEP_BINS + i).start(priority=i % 2)

    def wait_body(place, carry):
        write(place).wait()
        return carry

    lax.fori_loop(0, BIN, wait_body, 0)


def per_device_kernels(records, quality, block_ids):
    devices = lax.axis_size("rcv")
    groups = devices // NB
    windows, channels, samples = records.shape
    sub_rows = channels // groups
    pack = LANES // sub_rows
    planes = devices // pack
    rows = 2 * BIN
    depth = windows * rows
    table = basis_table(samples, samples // 2).reshape(samples // 2, 2, NB * BIN)
    basis = jnp.asarray(np.ascontiguousarray(table.transpose(1, 0, 2)))
    padded_ids = jnp.pad(block_ids.reshape(1, -1), ((0, windows - 1), (0, LANES - channels - NSB)))
    small = jnp.concatenate([quality, padded_ids], axis=1)
    rhs, src = pl.pallas_call(
        exchange_kernel,
        out_shape=(
            jax.ShapeDtypeStruct((2, planes, depth, LANES), jnp.bfloat16),
            jax.ShapeDtypeStruct((groups, NSB, sub_rows, depth), jnp.bfloat16),
        ),
        in_specs=[
            pl.BlockSpec(memory_space=pltpu.VMEM),
            pl.BlockSpec(memory_space=pltpu.HBM),
            pl.BlockSpec(memory_space=pltpu.HBM),
        ],
        out_specs=(pl.BlockSpec(memory_space=pltpu.VMEM), pl.BlockSpec(memory_space=pltpu.VMEM)),
        scratch_shapes=[
            pltpu.VMEM(basis.shape, jnp.bfloat16),
            pltpu.VMEM((2, windows * channels, samples // 2), jnp.bfloat16),
            pltpu.VMEM((devices, rows, LANES), jnp.bfloat16),
            pltpu.VMEM((devices, rows, LANES), jnp.bfloat16),
            pltpu.VMEM((NSB, sub_rows, depth), jnp.bfloat16),
            pltpu.SemaphoreType.DMA((2 * groups * windows,)),
            pltpu.SemaphoreType.DMA((2,)),
            pltpu.SemaphoreType.DMA((devices,)),
            pltpu.SemaphoreType.DMA((devices,)),
            pltpu.SemaphoreType.DMA((2,)),
        ],
        compiler_params=pltpu.CompilerParams(
            collective_id=0, has_side_effects=True, vmem_limit_bytes=53 * 2**20
        ),
        name="spectra_exchange",
    )(small, basis, records)

    count = NSB * SBLK
    out_shape = (BIN, count, 2 * planes * LANES)
    joined = pl.pallas_call(
        product_kernel,
        out_shape=jax.ShapeDtypeStruct(out_shape, jnp.bfloat16),
        in_specs=[pl.BlockSpec(memory_space=pltpu.VMEM)] * 2,
        out_specs=pl.BlockSpec(memory_space=pltpu.HBM),
        scratch_shapes=[
            pltpu.VMEM((count, depth), jnp.float32),
            pltpu.VMEM(out_shape, jnp.bfloat16),
            pltpu.SemaphoreType.DMA((BIN,)),
        ],
        compiler_params=pltpu.CompilerParams(vmem_limit_bytes=40 * 2**20),
        name="cross_spectra",
    )(src, rhs)
    return joined[None]


def make_basis(samples):
    return jnp.asarray(basis_table(samples, samples))


def from_partner(value, axis, stride):
    mask = 2**stride
    pairs = [(source, source ^ mask) for source in range(lax.axis_size(axis))]
    return lax.ppermute(value, axis, pairs)


def per_device_general(records, quality, block_ids):
    devices = lax.axis_size("rcv")
    groups = devices // NB
    windows, channels, samples = records.shape
    sub_rows = channels // groups
    basis_table = make_basis(samples).reshape(samples, NB, 2 * BIN)
    rec_rows = records.reshape(windows, groups, sub_rows, samples)
    spectrum = jnp.einsum(
        "wqjs,sbm->bqwjm", rec_rows, basis_table, preferred_element_type=jnp.float32
    )
    band_power = jnp.sum(spectrum * spectrum, axis=-1) / BIN
    keep_gate = quality.reshape(windows, groups, sub_rows).transpose(1, 0, 2).astype(jnp.float32)
    scaling = keep_gate[None] * lax.rsqrt(band_power + 1e-05)
    whitened = (spectrum * scaling[..., None]).astype(jnp.bfloat16)
    send_buf = whitened.reshape(devices, windows, sub_rows * 2 * BIN)
    arrived = lax.all_to_all(send_buf, "rcv", split_axis=0, concat_axis=0, tiled=True)
    receivers = arrived.reshape(devices, windows, sub_rows, 2, BIN)
    my_index = lax.axis_index("rcv")
    per_block = channels // SBLK
    blk_rows = SBLK // sub_rows
    own_pieces = []
    for source_slot in range(NSB):
        owner_dev = block_ids[source_slot] // per_block
        own_pieces.append(lax.dynamic_index_in_dim(arrived, owner_dev, 0, keepdims=False))
    collected = jnp.stack(own_pieces)[None]
    my_group = my_index % groups
    for bit_level in range(groups.bit_length() - 1):
        partner = from_partner(collected, "rcv", bit_level)
        upper_side = my_group // 2**bit_level % 2 == 1
        low_half = jnp.where(upper_side, partner, collected)
        high_half = jnp.where(upper_side, collected, partner)
        collected = jnp.concatenate([low_half, high_half], axis=0)
    slices = []
    for source_slot in range(NSB):
        slices.append(collected[:, source_slot])
    src_band = jnp.stack(slices).reshape(NSB, blk_rows, windows, sub_rows, 2, BIN)
    source_count = NSB * SBLK
    group_width = devices * sub_rows
    left_side = src_band.transpose(5, 0, 1, 3, 2, 4).reshape(BIN, source_count, windows, 2)
    rec_cols = receivers.transpose(4, 1, 3, 0, 2).reshape(BIN, windows, 2, group_width)
    rotated = jnp.stack([rec_cols[:, :, 1], -rec_cols[:, :, 0]], axis=2)
    right_side = jnp.concatenate([rec_cols, rotated], axis=-1)
    joined = jnp.einsum("inwp,iwpk->ink", left_side, right_side, preferred_element_type=jnp.float32)
    return (joined * (1.0 / windows)).astype(jnp.bfloat16)[None]


def per_device(records, quality, block_ids):
    devices = lax.axis_size("rcv")
    windows, channels, samples = records.shape
    groups = devices // NB
    sub_rows = channels // groups
    pack = LANES // sub_rows
    fits = (
        groups == 2
        and channels == SBLK
        and windows == pack
        and sub_rows * pack == LANES
        and NSB * groups == pack
        and devices % (2 * pack) == 0
        and FLO % 2 == 0
        and samples % 2 == 0
    )
    return (per_device_kernels if fits else per_device_general)(records, quality, block_ids)


def solution(mesh):
    placed = (P("grp", "rcv", None), P("grp", "rcv"), P("grp"))
    return jax.shard_map(
        per_device,
        mesh=mesh,
        in_specs=placed,
        out_specs=P("rcv", "grp", None, None),
        check_vma=False,
    )
```

```python
import functools

import jax
import jax.numpy as jnp
import ml_dtypes
import numpy as np
from jax import lax
from jax.experimental import pallas as pl
from jax.experimental.pallas import tpu as pltpu
from jax.sharding import PartitionSpec as P

NB = 8
BIN = 32
FLO = 64
SBLK = 64
NSB = 2
LANES = 128


def basis_table(samples, count):
    times = np.arange(count, dtype=np.int64)
    bins = FLO + np.arange(NB * BIN, dtype=np.int64)
    phases = (times[:, None] * bins[None, :]) % samples
    angles = phases.astype(np.float64) * (2.0 * np.pi / samples)
    table = np.stack([np.cos(angles), -np.sin(angles)]).reshape(2, count, NB, BIN)
    table = table.transpose(1, 2, 0, 3).reshape(count, NB * 2 * BIN)
    return table.astype(np.float32).astype(ml_dtypes.bfloat16)


def lanes_to_rows(pieces, width):
    lane = lax.broadcasted_iota(jnp.int32, pieces[0].shape, 1) // width
    wide = [piece.astype(jnp.float32) for piece in pieces]
    result = []
    for w in range(len(pieces)):
        total = None
        for e, piece in enumerate(wide):
            shift = (e - w) * width % LANES
            moved = pltpu.roll(piece, shift, 1) if shift else piece
            total = moved if total is None else jnp.where(lane == e, moved, total)
        result.append(total)
    return result


def flipped(me, off):
    other, bit = me, 1
    while bit <= off:
        if off & bit:
            other = other + bit * (1 - 2 * (me // bit % 2))
        bit *= 2
    return other


def exchange_kernel(
    small_ref, basis_ref, records_ref, rhs_ref, src_ref,
    basis_v, rec_v, send_v, recv_v, own_v,
    load_sem, basis_sem, send_sem, recv_sem, src_sem,
):
    devices = recv_v.shape[0]
    windows, channels, samples = records_ref.shape
    groups = devices // NB
    sub_rows = channels // groups
    pack = LANES // sub_rows
    planes = devices // pack
    half = samples // 2
    rows = 2 * BIN
    me = lax.axis_index("rcv")

    barrier = pltpu.get_barrier_semaphore()
    for off in range(1, devices):
        pl.semaphore_signal(
            barrier, inc=1, device_id={"rcv": flipped(me, off)},
            device_id_type=pl.DeviceIdType.MESH,
        )

    near_side = me // (devices // 2)
    sides = (1 - near_side, near_side)
    basis_loads = [
        pltpu.make_async_copy(basis_ref.at[side], basis_v.at[turn], basis_sem.at[turn])
        for turn, side in enumerate(sides)
    ]
    loads = []
    for q in range(groups):
        loads.append([])
        for w in range(windows):
            for h in range(2):
                loads[q].append(
                    pltpu.make_async_copy(
                        records_ref.at[w, pl.ds(q * sub_rows, sub_rows), pl.ds(h * half, half)],
                        rec_v.at[q, h, pl.ds(w * sub_rows, sub_rows)],
                        load_sem.at[q, 2 * w + h],
                    )
                )
    basis_loads[0].start()
    for group_loads in loads:
        for turn, load in enumerate(group_loads):
            load.start(priority=turn % 2)
    basis_loads[1].start()

    def remote(peer):
        return pltpu.make_async_remote_copy(
            src_ref=send_v.at[peer], dst_ref=recv_v.at[me],
            send_sem=send_sem.at[peer], recv_sem=recv_sem.at[me],
            device_id={"rcv": peer}, device_id_type=pl.DeviceIdType.MESH,
        )

    def arrival(peer):
        return pltpu.make_async_remote_copy(
            src_ref=send_v.at[peer], dst_ref=recv_v.at[peer],
            send_sem=send_sem.at[peer], recv_sem=recv_sem.at[peer],
            device_id={"rcv": peer}, device_id_type=pl.DeviceIdType.MESH,
        )

    my_plane, my_place = me // pack, me % pack
    far_planes = [
        near_side * u + (1 - near_side) * (planes - 1 - u) for u in range(planes // 2)
    ]
    near_planes = [flipped(my_plane, u) for u in range(planes // 2 - 1, -1, -1)]
    odd = lax.broadcasted_iota(jnp.int32, (LANES, NB * BIN), 1) % 2 == 1
    for turn, side in enumerate(sides):
        basis_loads[turn].wait()
        for q in range(groups):
            if turn == 0:
                for load in loads[q]:
                    load.wait()
            keep = jnp.concatenate(
                [small_ref[w : w + 1, q * sub_rows : (q + 1) * sub_rows] for w in range(windows)],
                axis=1,
            ).astype(jnp.float32)
            halves = jnp.dot(
                rec_v[q].reshape(2 * LANES, half), basis_v[turn], preferred_element_type=jnp.float32
            )
            late = halves[LANES:]
            spectra = (halves[:LANES] + jnp.where(odd, -late, late)).T
            for b in range(NB // 2):
                spectrum = spectra[b * rows : (b + 1) * rows]
                power = jnp.sum(spectrum * spectrum, axis=0, keepdims=True) / BIN
                white = spectrum * (keep * lax.rsqrt(power + 1e-05))
                send_v[side * (devices // 2) + b * groups + q] = white.astype(jnp.bfloat16)
            if turn == 0 and q == 0:
                pl.semaphore_wait(barrier, devices - 1)
            for plane in far_planes[:1] if turn == 0 else near_planes:
                for v in range(pack // groups - 1, -1, -1):
                    peer = plane * pack + flipped(my_place // groups, v) * groups + q
                    if turn == 1 and plane is near_planes[-1] and v == 0:
                        pl.when(me % groups != q)(remote(peer).start)
                    else:
                        remote(peer).start()
        if turn == 0:
            for plane in far_planes[1:]:
                for e in range(pack - 1, -1, -1):
                    remote(plane * pack + flipped(my_place, e)).start()
    recv_v[me] = send_v[me]

    ordered = near_planes[::-1] + far_planes
    for turn, plane in enumerate(ordered):
        for e in range(0 if turn else 1, pack):
            arrival(plane * pack + flipped(my_place, e)).wait_recv()
        if turn == planes - 1:
            for s in range(NSB):
                turned = recv_v[small_ref[0, channels + s]].astype(jnp.float32).T * (1.0 / windows)
                own_v[s] = jnp.concatenate(
                    [turned[w * sub_rows : (w + 1) * sub_rows] for w in range(windows)], axis=1
                ).astype(jnp.bfloat16)
            swap = pltpu.make_async_remote_copy(
                src_ref=own_v, dst_ref=src_ref.at[me % groups],
                send_sem=src_sem.at[0], recv_sem=src_sem.at[1],
                device_id={"rcv": flipped(me, 1)}, device_id_type=pl.DeviceIdType.MESH,
            )
            swap.start()
            src_ref[me % groups] = own_v[...]
        by_window = lanes_to_rows([recv_v[plane * pack + e] for e in range(pack)], sub_rows)
        for w, block in enumerate(by_window):
            real, imag = block[:BIN], block[BIN:]
            rhs_ref[0, plane, w * rows : w * rows + BIN] = real.astype(jnp.bfloat16)
            rhs_ref[0, plane, w * rows + BIN : (w + 1) * rows] = imag.astype(jnp.bfloat16)
            rhs_ref[1, plane, w * rows : w * rows + BIN] = imag.astype(jnp.bfloat16)
            rhs_ref[1, plane, w * rows + BIN : (w + 1) * rows] = (-real).astype(jnp.bfloat16)
    for off in range(1, devices):
        remote(flipped(me, off)).wait_send()
    swap.wait()


STEP_BINS = 2


def product_kernel(src_ref, rhs_ref, out_ref, left_v, out_v, out_sem):
    planes = rhs_ref.shape[1]
    groups, blocks = src_ref.shape[:2]
    wide = 2

    left_v[...] = jnp.concatenate(
        [src_ref[q, s].astype(jnp.float32) for s in range(blocks) for q in range(groups)], axis=0
    )

    def write(place):
        return pltpu.make_async_copy(out_v.at[place], out_ref.at[place], out_sem.at[place])

    for step in range(BIN // STEP_BINS):
        left = left_v[...]
        bin_of = lax.broadcasted_iota(jnp.int32, left.shape, 1) % BIN
        masked = jnp.concatenate(
            [
                jnp.where(bin_of == step * STEP_BINS + i, left, 0.0).astype(jnp.bfloat16)
                for i in range(STEP_BINS)
            ],
            axis=0,
        )
        for part in range(2):
            for z in range(0, planes, wide):
                right = jnp.concatenate([rhs_ref[part, z + u] for u in range(wide)], axis=1)
                both = jnp.dot(masked, right, preferred_element_type=jnp.float32)
                first = (part * planes + z) * LANES
                out_v[pl.ds(step * STEP_BINS, STEP_BINS), :, first : first + wide * LANES] = (
                    both.astype(jnp.bfloat16).reshape(STEP_BINS, left.shape[0], wide * LANES)
                )
        for i in range(STEP_BINS):
            write(step * STEP_BINS + i).start(priority=i % 2)

    def wait_body(place, carry):
        write(place).wait()
        return carry

    lax.fori_loop(0, BIN, wait_body, 0)


def per_device_kernels(records, quality, block_ids):
    devices = lax.axis_size("rcv")
    groups = devices // NB
    windows, channels, samples = records.shape
    sub_rows = channels // groups
    pack = LANES // sub_rows
    planes = devices // pack
    rows = 2 * BIN
    depth = windows * rows
    table = basis_table(samples, samples // 2).reshape(samples // 2, 2, NB * BIN)
    basis = jnp.asarray(np.ascontiguousarray(table.transpose(1, 0, 2)))
    padded_ids = jnp.pad(block_ids.reshape(1, -1), ((0, windows - 1), (0, LANES - channels - NSB)))
    small = jnp.concatenate([quality, padded_ids], axis=1)
    rhs, src = pl.pallas_call(
        exchange_kernel,
        out_shape=(
            jax.ShapeDtypeStruct((2, planes, depth, LANES), jnp.bfloat16),
            jax.ShapeDtypeStruct((groups, NSB, sub_rows, depth), jnp.bfloat16),
        ),
        in_specs=[
            pl.BlockSpec(memory_space=pltpu.VMEM),
            pl.BlockSpec(memory_space=pltpu.HBM),
            pl.BlockSpec(memory_space=pltpu.HBM),
        ],
        out_specs=(pl.BlockSpec(memory_space=pltpu.VMEM), pl.BlockSpec(memory_space=pltpu.VMEM)),
        scratch_shapes=[
            pltpu.VMEM(basis.shape, jnp.bfloat16),
            pltpu.VMEM((groups, 2, LANES, samples // 2), jnp.bfloat16),
            pltpu.VMEM((devices, rows, LANES), jnp.bfloat16),
            pltpu.VMEM((devices, rows, LANES), jnp.bfloat16),
            pltpu.VMEM((NSB, sub_rows, depth), jnp.bfloat16),
            pltpu.SemaphoreType.DMA((groups, 2 * windows)),
            pltpu.SemaphoreType.DMA((2,)),
            pltpu.SemaphoreType.DMA((devices,)),
            pltpu.SemaphoreType.DMA((devices,)),
            pltpu.SemaphoreType.DMA((2,)),
        ],
        compiler_params=pltpu.CompilerParams(
            collective_id=0, has_side_effects=True, vmem_limit_bytes=53 * 2**20
        ),
        name="spectra_exchange",
    )(small, basis, records)

    count = NSB * SBLK
    out_shape = (BIN, count, 2 * planes * LANES)
    joined = pl.pallas_call(
        product_kernel,
        out_shape=jax.ShapeDtypeStruct(out_shape, jnp.bfloat16),
        in_specs=[pl.BlockSpec(memory_space=pltpu.VMEM)] * 2,
        out_specs=pl.BlockSpec(memory_space=pltpu.HBM),
        scratch_shapes=[
            pltpu.VMEM((count, depth), jnp.float32),
            pltpu.VMEM(out_shape, jnp.bfloat16),
            pltpu.SemaphoreType.DMA((BIN,)),
        ],
        compiler_params=pltpu.CompilerParams(vmem_limit_bytes=40 * 2**20),
        name="cross_spectra",
    )(src, rhs)
    return joined[None]


def make_basis(samples):
    return jnp.asarray(basis_table(samples, samples))


def from_partner(value, axis, stride):
    mask = 2**stride
    pairs = [(source, source ^ mask) for source in range(lax.axis_size(axis))]
    return lax.ppermute(value, axis, pairs)


def per_device_general(records, quality, block_ids):
    devices = lax.axis_size("rcv")
    groups = devices // NB
    windows, channels, samples = records.shape
    sub_rows = channels // groups
    basis_table = make_basis(samples).reshape(samples, NB, 2 * BIN)
    rec_rows = records.reshape(windows, groups, sub_rows, samples)
    spectrum = jnp.einsum(
        "wqjs,sbm->bqwjm", rec_rows, basis_table, preferred_element_type=jnp.float32
    )
    band_power = jnp.sum(spectrum * spectrum, axis=-1) / BIN
    keep_gate = quality.reshape(windows, groups, sub_rows).transpose(1, 0, 2).astype(jnp.float32)
    scaling = keep_gate[None] * lax.rsqrt(band_power + 1e-05)
    whitened = (spectrum * scaling[..., None]).astype(jnp.bfloat16)
    send_buf = whitened.reshape(devices, windows, sub_rows * 2 * BIN)
    arrived = lax.all_to_all(send_buf, "rcv", split_axis=0, concat_axis=0, tiled=True)
    receivers = arrived.reshape(devices, windows, sub_rows, 2, BIN)
    my_index = lax.axis_index("rcv")
    per_block = channels // SBLK
    blk_rows = SBLK // sub_rows
    own_pieces = []
    for source_slot in range(NSB):
        owner_dev = block_ids[source_slot] // per_block
        own_pieces.append(lax.dynamic_index_in_dim(arrived, owner_dev, 0, keepdims=False))
    collected = jnp.stack(own_pieces)[None]
    my_group = my_index % groups
    for bit_level in range(groups.bit_length() - 1):
        partner = from_partner(collected, "rcv", bit_level)
        upper_side = my_group // 2**bit_level % 2 == 1
        low_half = jnp.where(upper_side, partner, collected)
        high_half = jnp.where(upper_side, collected, partner)
        collected = jnp.concatenate([low_half, high_half], axis=0)
    slices = []
    for source_slot in range(NSB):
        slices.append(collected[:, source_slot])
    src_band = jnp.stack(slices).reshape(NSB, blk_rows, windows, sub_rows, 2, BIN)
    source_count = NSB * SBLK
    group_width = devices * sub_rows
    left_side = src_band.transpose(5, 0, 1, 3, 2, 4).reshape(BIN, source_count, windows, 2)
    rec_cols = receivers.transpose(4, 1, 3, 0, 2).reshape(BIN, windows, 2, group_width)
    rotated = jnp.stack([rec_cols[:, :, 1], -rec_cols[:, :, 0]], axis=2)
    right_side = jnp.concatenate([rec_cols, rotated], axis=-1)
    joined = jnp.einsum("inwp,iwpk->ink", left_side, right_side, preferred_element_type=jnp.float32)
    return (joined * (1.0 / windows)).astype(jnp.bfloat16)[None]


def per_device(records, quality, block_ids):
    devices = lax.axis_size("rcv")
    windows, channels, samples = records.shape
    groups = devices // NB
    sub_rows = channels // groups
    pack = LANES // sub_rows
    fits = (
        groups == 2
        and channels == SBLK
        and windows == pack
        and sub_rows * pack == LANES
        and NSB * groups == pack
        and devices % (2 * pack) == 0
        and FLO % 2 == 0
        and samples % 2 == 0
    )
    return (per_device_kernels if fits else per_device_general)(records, quality, block_ids)


def solution(mesh):
    placed = (P("grp", "rcv", None), P("grp", "rcv"), P("grp"))
    return jax.shard_map(
        per_device,
        mesh=mesh,
        in_specs=placed,
        out_specs=P("rcv", "grp", None, None),
        check_vma=False,
    )
```
